256 devices in a mesh: tile: 16 (over y_lo, x, core), tracer: 16 (over y_hi, z).
Axes of the slice: x: 4, y: 4 (y_hi: 2, y_lo: 2; y = y_hi * 2 + y_lo), z: 8, core: 2. Of those that a mesh axis runs over, the one named last changes fastest.
Arguments:
- tracers: float32 [32, 24, 512, 256], P('tracer', None, 'tile'), may hold values from 0.1 to 4
- east_speed: float32 [24, 512, 256], P(None, 'tile'), may hold values from -2.5 to 2.5
- north_speed: float32 [24, 512, 256], P(None, 'tile'), may hold values from -2.5 to 2.5
- land_mask: int32 [512, 256], P('tile'), may hold values 0 or 1
- bottom_level: int32 [512, 256], P('tile'), may hold values from 1 to 24
- in_weight: bfloat16 [32, 512], replicated, may hold values from -1 to 1
- in_bias: float32 [512], replicated, may hold values from -4 to 4
- mid_weight: bfloat16 [512, 512], replicated, may hold values from -0.25 to 0.25
- mid_bias: float32 [512], replicated, may hold values from -4 to 4
- out_weight: bfloat16 [512, 32], replicated, may hold values from -0.25 to 0.25
Outputs:
- advanced: float32 [32, 24, 512, 256], P('tracer', None, 'tile')
The draws below stay inside these ranges and needn't reach their ends.
All inputs are finite; a program needn't handle non-finite values. No bound on the sum of `land_mask` on one device may be relied on, other than what follows from the above.
Results may differ from the reference program's by a relative error of at most 0.002.
Values may be sent and summed in bfloat16 or wider, within the bound.
No kernel may reach another device: no remote copies, remote signals or barrier semaphores. Data moves between devices by JAX's collectives and lax.ppermute only.
A program may use at most 192 MiB of HBM per device.

```python
import math
import jax
import jax.numpy as jnp
from jax import lax

TRACERS = 32
HIDDEN_SIZE = 512
LEVELS = 24
COLUMNS = 256
STEPS = 2
SLAB_ROWS = 512


def plant(entries, key, smallest, high):
    extent = entries.shape
    place = [jax.random.randint(jax.random.fold_in(key, axis), (), 0, extent[axis]) for axis in range(len(extent))]
    entries = entries.at[tuple(place)].set(smallest)
    longest = extent.index(max(extent))
    place[longest] = (place[longest] + 1) % extent[longest]
    return entries.at[tuple(place)].set(high)


def block_scale(own_key, extent, cuts, least, top_value):
    def one(position, parts):
        steps = jax.random.uniform(jax.random.fold_in(jax.random.fold_in(own_key, 6), position), (parts,), jnp.float32, least / len(cuts), top_value / len(cuts))
        return jnp.repeat(jnp.exp(steps), extent[position] // parts).reshape((-1,) + (1,) * (len(extent) - position - 1))

    level = one(*cuts[0])
    for cut in cuts[1:]:
        level = level * one(*cut)
    return level


def gaussian(own_key, dims, spread, bound, split=(), kind=jnp.bfloat16):
    values = jax.random.normal(own_key, dims, jnp.float32) * spread
    if len(split) > 0:
        values = block_scale(own_key, dims, split, -0.22, 0.18) * values
    return jnp.clip(values, min=-bound, max=bound).astype(kind)


def setup_inputs(seed: int = 0) -> dict:
    key_list = jax.random.split(jax.random.key(seed), 11)
    return {
        "tracers": jnp.clip(jnp.exp(math.log(4.0) - 3.6888794 * jax.random.uniform(key_list[0], (TRACERS, LEVELS, SLAB_ROWS, COLUMNS), jnp.float32) ** block_scale(key_list[0], (TRACERS, LEVELS, SLAB_ROWS, COLUMNS), ((0, 16), (2, 16)), -0.2, 0.2)), 0.1, 4.0),
        "east_speed": gaussian(key_list[1], (LEVELS, SLAB_ROWS, COLUMNS), 0.4, 2.5, ((1, 16),), jnp.float32),
        "north_speed": gaussian(key_list[2], (LEVELS, SLAB_ROWS, COLUMNS), 0.4, 2.5, ((1, 16),), jnp.float32),
        "land_mask": plant((jax.random.randint(key_list[3], (SLAB_ROWS, COLUMNS), 0, 5) < 4).astype(jnp.int32), jax.random.fold_in(key_list[3], 1), 0, 1),
        "bottom_level": plant(jax.random.randint(key_list[4], (SLAB_ROWS, COLUMNS), 1, LEVELS + 1), jax.random.fold_in(key_list[4], 1), 1, LEVELS).astype(jnp.int32),
        "in_weight": gaussian(key_list[5], (TRACERS, HIDDEN_SIZE), TRACERS ** -0.5, 1.0),
        "in_bias": gaussian(key_list[6], (HIDDEN_SIZE,), 1.0, 4.0, (), jnp.float32),
        "mid_weight": gaussian(key_list[7], (HIDDEN_SIZE, HIDDEN_SIZE), HIDDEN_SIZE ** -0.5, 0.25),
        "mid_bias": gaussian(key_list[8], (HIDDEN_SIZE,), 1.0, 4.0, (), jnp.float32),
        "out_weight": gaussian(key_list[9], (HIDDEN_SIZE, TRACERS), HIDDEN_SIZE ** -0.5, 0.25),
    }


diffusion = 0.2
time_step = 0.2


def wet_field(land_mask, bottom_level):
    levels = jnp.arange(LEVELS, dtype=jnp.int32)[:, None, None]
    return ((land_mask[None] == 1) & (levels < bottom_level[None])).astype(jnp.float32)


def face_flux(behind_cells, ahead_cells, flow_speed, opened):
    moved = jnp.maximum(flow_speed, 0.0) * behind_cells + jnp.minimum(flow_speed, 0.0) * ahead_cells
    return opened * (moved - diffusion * (ahead_cells - behind_cells))


def transport(field, east_speed, north_speed, wet_cells):
    cells_x = jnp.pad(field, ((0, 0), (0, 0), (1, 1), (0, 0)))
    flow_x = jnp.pad(east_speed, ((0, 0), (1, 1), (0, 0)))
    wet_x = jnp.pad(wet_cells, ((0, 0), (1, 1), (0, 0)))
    x_flux = face_flux(cells_x[:, :, :-1], cells_x[:, :, 1:], flow_x[:, :-1], wet_x[:, :-1] * wet_x[:, 1:])
    cells_y = jnp.pad(field, ((0, 0), (0, 0), (0, 0), (1, 1)))
    flow_y = jnp.pad(north_speed, ((0, 0), (0, 0), (1, 1)))
    wet_y = jnp.pad(wet_cells, ((0, 0), (0, 0), (1, 1)))
    y_flux = face_flux(cells_y[..., :-1], cells_y[..., 1:], flow_y[..., :-1], wet_y[..., :-1] * wet_y[..., 1:])
    return (x_flux[:, :, :-1] - x_flux[:, :, 1:]) + (y_flux[..., :-1] - y_flux[..., 1:])


def source_terms(field, in_weight, in_bias, mid_weight, mid_bias, out_weight):
    inputs = jnp.moveaxis(field.astype(jnp.bfloat16), 1, 0)

    def one_level(slab_level):
        first_hidden = jnp.einsum('txy,th->xyh', slab_level.astype(jnp.float32), in_weight.astype(jnp.float32)) + in_bias
        first_hidden = jax.nn.silu(first_hidden).astype(jnp.bfloat16)
        second_hidden = jnp.einsum('xyh,hk->xyk', first_hidden.astype(jnp.float32), mid_weight.astype(jnp.float32)) + mid_bias
        second_hidden = jax.nn.silu(second_hidden).astype(jnp.bfloat16)
        return jnp.einsum('xyh,ht->txy', second_hidden.astype(jnp.float32), out_weight.astype(jnp.float32)).astype(jnp.bfloat16)

    return jnp.moveaxis(lax.map(one_level, inputs), 0, 1)


def reference(tracers, east_speed, north_speed, land_mask, bottom_level, in_weight, in_bias, mid_weight, mid_bias, out_weight):
    wet_cells = wet_field(land_mask, bottom_level)
    field = tracers
    for step in range(STEPS):
        sources = source_terms(field, in_weight, in_bias, mid_weight, mid_bias, out_weight)
        tendency = transport(field, east_speed, north_speed, wet_cells)
        field = wet_cells[None] * (field + time_step * (tendency + sources.astype(jnp.float32)))
    return field
```

```python
import functools

import jax
import jax.numpy as jnp
from jax import lax
from jax.experimental import pallas as pl
from jax.experimental.pallas import tpu as pltpu
from jax.sharding import PartitionSpec as P

STEPS = 2
diffusion = 0.2
time_step = 0.2
GROUP = 4

BF16 = jnp.bfloat16
F32 = jnp.float32


def silu_of_half(half):
    return (half + half * jnp.tanh(half)).astype(BF16)


def network(cells, in_weight, mid_weight, mid_bias, out_weight):
    lanes = cells.shape[1]
    cells = jnp.concatenate([cells, jnp.ones((16, lanes), BF16)], axis=0)
    hidden = silu_of_half(jnp.dot(in_weight, cells, preferred_element_type=F32))
    hidden = jnp.dot(mid_weight, hidden, preferred_element_type=F32)
    hidden = silu_of_half(hidden + jnp.concatenate([mid_bias] * (lanes // 128), axis=1))
    return jnp.dot(out_weight, hidden, preferred_element_type=F32)


def turn_kernel(rows, x_ref, turned_ref, first_ref, last_ref, scratch):
    kinds, levels = x_ref.shape[:2]
    for level in range(levels):
        for part in range(scratch.shape[0]):
            block = x_ref[:, level, :, part * 128 : (part + 1) * 128]
            scratch[part] = block.astype(F32).reshape(kinds * rows, 128)
        for row in range(rows):
            picked = [scratch[part, pl.ds(row, kinds, stride=rows), :] for part in range(scratch.shape[0])]
            piece = jnp.concatenate(picked, axis=1).astype(BF16)
            turned_ref[level * rows + row] = piece
            if row < 2:
                first_ref[level * 2 + row] = piece
            if row >= rows - 2:
                last_ref[level * 2 + row - rows + 2] = piece


def source_kernel(cells_ref, in_ref, mid_ref, bias_ref, out_ref, sources_ref):
    def body(i, _):
        cells = jnp.concatenate([cells_ref[i * GROUP + k] for k in range(GROUP)], axis=1)
        result = network(cells, in_ref[...], mid_ref[...], bias_ref[...], out_ref[...])
        width = cells_ref.shape[2]
        for k in range(GROUP):
            sources_ref[i * GROUP + k] = result[:, k * width : (k + 1) * width].astype(BF16)
        return 0

    lax.fori_loop(0, cells_ref.shape[0] // GROUP, body, 0)


def advance(here, above, below, sources, factors):
    width = here.shape[1]
    west = pltpu.roll(here, 1, 1)
    east = pltpu.roll(here, width - 1, 1)
    result = factors[0:1] * here + factors[1:2] * above + factors[2:3] * below
    return result + factors[3:4] * west + factors[4:5] * east + factors[5:6] * sources


def step_kernel(
    rows,
    cells_ref,
    sources_ref,
    top_ref,
    bottom_ref,
    factors_ref,
    in_ref,
    mid_ref,
    bias_ref,
    out_ref,
    change_ref,
    wide,
    wide_sources,
    middle,
    scratch,
):
    levels = cells_ref.shape[0] // rows
    width = cells_ref.shape[2]
    ahead, wider = rows + 2, rows + 4
    edge = []
    for level in range(levels):
        edge += [top_ref[level * 2 + 1], bottom_ref[level * 2]]
    result = network(
        jnp.concatenate(edge, axis=1), in_ref[...], mid_ref[...], bias_ref[...], out_ref[...]
    ).astype(BF16).astype(F32)
    for level in range(levels):
        at = 2 * level * width
        wide_sources[level * ahead] = result[:, at : at + width]
        wide_sources[level * ahead + ahead - 1] = result[:, at + width : at + 2 * width]
        for k in range(2):
            wide[level * wider + k] = top_ref[level * 2 + k].astype(F32)
            wide[level * wider + rows + 2 + k] = bottom_ref[level * 2 + k].astype(F32)

        def widen(row, _):
            wide[level * wider + 2 + row] = cells_ref[level * rows + row].astype(F32)
            wide_sources[level * ahead + 1 + row] = sources_ref[level * rows + row].astype(F32)
            return 0

        lax.fori_loop(0, rows, widen, 0, unroll=4)

        def first_step(row, _):
            at = level * wider + row
            middle[level * ahead + row] = advance(
                wide[at + 1],
                wide[at],
                wide[at + 2],
                wide_sources[level * ahead + row],
                factors_ref[level * ahead + row],
            )
            return 0

        lax.fori_loop(0, ahead, first_step, 0, unroll=3)

    turns = rows // GROUP

    def second_step(i, _):
        level = i // turns
        row = (i - level * turns) * GROUP
        at = level * ahead + row + 1
        held = [middle[at - 1 + k] for k in range(GROUP + 2)]
        cells = jnp.concatenate([held[k + 1].astype(BF16) for k in range(GROUP)], axis=1)
        result = network(cells, in_ref[...], mid_ref[...], bias_ref[...], out_ref[...])
        for k in range(GROUP):
            factors = factors_ref[at + k]
            value = advance(
                held[k + 1],
                held[k],
                held[k + 2],
                result[:, k * width : (k + 1) * width].astype(BF16).astype(F32),
                factors,
            )
            value = value - factors[6:7] * wide[level * wider + row + k + 2]
            kinds = value.shape[0]
            for part in range(scratch.shape[0]):
                scratch[part, pl.ds(level * rows * kinds + row + k, kinds, stride=rows), :] = value[
                    :, part * 128 : (part + 1) * 128
                ]
        return 0

    lax.fori_loop(0, levels * turns, second_step, 0)
    kinds = change_ref.shape[0]
    for level in range(levels):
        for part in range(scratch.shape[0]):
            block = scratch[part, level * rows * kinds : (level + 1) * rows * kinds, :]
            change_ref[:, level, :, part * 128 : (part + 1) * 128] = block.reshape(kinds, rows, 128).astype(BF16)


def kernel_call(kernel, outs, scratch, flops, name):
    return pl.pallas_call(
        kernel,
        out_shape=outs,
        scratch_shapes=scratch,
        cost_estimate=pl.CostEstimate(flops=flops, bytes_accessed=4_000_000, transcendentals=0),
        compiler_params=pltpu.CompilerParams(vmem_limit_bytes=48 * 2**20),
        name=name,
    )


def factors_of(east, north, depth, first_level, levels):
    level = first_level + jnp.arange(levels, dtype=jnp.int32)[:, None, None]
    wet = (level.astype(F32) < depth[None]).astype(F32)
    opened = time_step * wet[:, :-1] * wet[:, 1:]
    plus = opened * (jnp.maximum(east[:, :-1], 0.0) + diffusion)
    minus = opened * (jnp.minimum(east[:, :-1], 0.0) - diffusion)
    inner = wet[:, 1:-1]
    flow = jnp.pad(north[:, 1:-1], ((0, 0), (0, 0), (1, 0)))
    sides = jnp.pad(inner, ((0, 0), (0, 0), (1, 1)))
    opened = time_step * sides[..., :-1] * sides[..., 1:]
    right = opened * (jnp.maximum(flow, 0.0) + diffusion)
    left = opened * (jnp.minimum(flow, 0.0) - diffusion)
    own = inner + (minus[:, :-1] - plus[:, 1:]) + (left[..., :-1] - right[..., 1:])
    return jnp.stack(
        [
            own,
            plus[:, :-1],
            -minus[:, 1:],
            right[..., :-1],
            -left[..., 1:],
            time_step * inner,
            inner,
            jnp.zeros_like(inner),
        ],
        axis=2,
    )


def body(
    tracers,
    east_speed,
    north_speed,
    land_mask,
    bottom_level,
    in_weight,
    in_bias,
    mid_weight,
    mid_bias,
    out_weight,
):
    kinds, levels, length, columns = tracers.shape
    tiles, group = lax.axis_size("tile"), lax.axis_size("tracer")
    halves = 2
    stacks = group // halves
    depth_each, rows = levels // stacks, length // halves
    own = lax.axis_index("tracer")
    half, stack = own // stacks, own % stacks
    all_kinds = kinds * group
    pieces = depth_each * rows

    sent = tracers.astype(BF16).reshape(kinds, stacks, depth_each, halves, rows, columns)
    sent = sent.transpose(3, 1, 0, 2, 4, 5).reshape(group, kinds, depth_each, rows, columns)
    cells = lax.all_to_all(sent, "tracer", split_axis=0, concat_axis=0, tiled=True)
    cells = cells.reshape(all_kinds, depth_each, rows, columns)

    depth = jnp.where(land_mask == 1, bottom_level, 0).astype(F32)
    first_level = stack * depth_each
    east = lax.dynamic_slice_in_dim(east_speed, first_level, depth_each, 0)
    north = lax.dynamic_slice_in_dim(north_speed, first_level, depth_each, 0)
    geometry = jnp.concatenate([east, north, depth[None]], axis=0)

    def at(tile, part, place):
        return tile * group + part * stacks + place

    across, back, within = [], [], []
    for place in range(stacks):
        for tile in range(tiles):
            within.append((at(tile, 0, place), at(tile, 1, place)))
            if tile + 1 < tiles:
                across.append((at(tile, 1, place), at(tile + 1, 0, place)))
    back = [(j, i) for i, j in across]
    axes = ("tile", "tracer")
    edge = lax.dynamic_slice_in_dim(geometry, half * (length - 2), 2, 1)
    arrived = lax.ppermute(edge, axes, across + back)
    geometry = jnp.where(
        half == 0,
        jnp.concatenate([arrived, geometry[:, : rows + 2]], axis=1),
        jnp.concatenate([geometry[:, rows - 2 :], arrived], axis=1),
    )
    factors = factors_of(
        geometry[:depth_each],
        geometry[depth_each : 2 * depth_each],
        geometry[2 * depth_each],
        first_level,
        depth_each,
    ).reshape(depth_each * (rows + 2), 8, columns)

    def parts(value):
        high = value.astype(BF16)
        low = (value - high.astype(F32)).astype(BF16)
        return [high, low, (value - high.astype(F32) - low.astype(F32)).astype(BF16)]

    in_parts = jnp.stack(parts(0.5 * in_bias) + [jnp.zeros(in_bias.shape, BF16)] * 13, axis=1)
    weights = (
        jnp.concatenate([(0.5 * in_weight.astype(F32)).astype(BF16).T, in_parts], axis=1),
        (0.5 * mid_weight.astype(F32)).astype(BF16).T,
        jnp.broadcast_to(0.5 * mid_bias[:, None], mid_bias.shape + (128,)),
        out_weight.T,
    )

    hidden = in_weight.shape[1]
    per_piece = 2 * columns * hidden * (hidden + 2 * all_kinds)
    turned, first, last = kernel_call(
        functools.partial(turn_kernel, rows),
        [
            jax.ShapeDtypeStruct((pieces, all_kinds, columns), BF16),
            jax.ShapeDtypeStruct((depth_each * 2, all_kinds, columns), BF16),
            jax.ShapeDtypeStruct((depth_each * 2, all_kinds, columns), BF16),
        ],
        [pltpu.VMEM((columns // 128, all_kinds * rows, 128), F32)],
        1_000_000,
        "turn",
    )(cells)
    top = lax.ppermute(last, axes, within + across)
    bottom = lax.ppermute(first, axes, [(j, i) for i, j in within] + back)
    sources = kernel_call(
        source_kernel,
        jax.ShapeDtypeStruct(turned.shape, BF16),
        [],
        pieces * per_piece,
        "sources",
    )(turned, *weights)
    change = kernel_call(
        functools.partial(step_kernel, rows),
        jax.ShapeDtypeStruct(cells.shape, BF16),
        [
            pltpu.VMEM((depth_each * (rows + 4), all_kinds, columns), F32),
            pltpu.VMEM((depth_each * (rows + 2), all_kinds, columns), F32),
            pltpu.VMEM((depth_each * (rows + 2), all_kinds, columns), F32),
            pltpu.VMEM((columns // 128, depth_each * rows * all_kinds, 128), F32),
        ],
        pieces * per_piece,
        "steps",
    )(turned, sources, top, bottom, factors, *weights)

    change = change.reshape(group, kinds, depth_each, rows, columns)
    change = lax.all_to_all(change, "tracer", split_axis=0, concat_axis=0, tiled=True)
    change = change.reshape(halves, stacks, kinds, depth_each, rows, columns)
    change = change.transpose(2, 1, 3, 0, 4, 5).reshape(kinds, levels, length, columns)
    level = jnp.arange(levels, dtype=jnp.int32)[:, None, None]
    wet = (level.astype(F32) < depth[None]).astype(F32)
    return wet[None] * (tracers + change.astype(F32))


def solution(mesh):
    return jax.shard_map(
        body,
        mesh=mesh,
        in_specs=(
            P("tracer", None, "tile", None),
            P(None, "tile", None),
            P(None, "tile", None),
            P("tile", None),
            P("tile", None),
            P(),
            P(),
            P(),
            P(),
            P(),
        ),
        out_specs=P("tracer", None, "tile", None),
        check_vma=False,
    )
```

```python
import functools

import jax
import jax.numpy as jnp
from jax import lax
from jax.experimental import pallas as pl
from jax.experimental.pallas import tpu as pltpu
from jax.sharding import PartitionSpec as P

STEPS = 2
diffusion = 0.2
time_step = 0.2
GROUP = 4
UNROLL = 1

BF16 = jnp.bfloat16
F32 = jnp.float32


def silu_of_half(half):
    return (half + half * jnp.tanh(half)).astype(BF16)


def network(cells, in_weight, mid_weight, mid_bias, out_weight):
    lanes = cells.shape[1]
    cells = jnp.concatenate([cells, jnp.ones((16, lanes), BF16)], axis=0)
    hidden = silu_of_half(jnp.dot(in_weight, cells, preferred_element_type=F32))
    hidden = jnp.dot(mid_weight, hidden, preferred_element_type=F32)
    hidden = silu_of_half(hidden + jnp.concatenate([mid_bias] * (lanes // 128), axis=1))
    return jnp.dot(out_weight, hidden, preferred_element_type=F32)


def turn_kernel(rows, x_ref, turned_ref, first_ref, last_ref, scratch):
    kinds, levels = x_ref.shape[:2]
    for level in range(levels):
        for part in range(scratch.shape[0]):
            block = x_ref[:, level, :, part * 128 : (part + 1) * 128]
            scratch[part] = block.astype(F32).reshape(kinds * rows, 128)
        for row in range(rows):
            picked = [scratch[part, pl.ds(row, kinds, stride=rows), :] for part in range(scratch.shape[0])]
            piece = jnp.concatenate(picked, axis=1).astype(BF16)
            turned_ref[level * rows + row] = piece
            if row < 2:
                first_ref[level * 2 + row] = piece
            if row >= rows - 2:
                last_ref[level * 2 + row - rows + 2] = piece


def source_kernel(rows, cells_ref, factors_ref, in_ref, mid_ref, bias_ref, out_ref, middle_ref):
    pieces, _, width = cells_ref.shape
    ahead, turns = rows + 2, rows // GROUP

    def body(i, _):
        level = i // turns
        row = (i - level * turns) * GROUP
        at = level * rows + row
        held = [cells_ref[jnp.maximum(at - 1, 0)]] + [cells_ref[at + k] for k in range(GROUP)]
        held.append(cells_ref[jnp.minimum(at + GROUP, pieces - 1)])
        cells = jnp.concatenate(held[1:-1], axis=1)
        result = network(cells, in_ref[...], mid_ref[...], bias_ref[...], out_ref[...])
        held = [value.astype(F32) for value in held]
        for k in range(GROUP):
            factors = factors_ref[level * ahead + row + 1 + k]
            above, below = factors[1:2], factors[2:3]
            if k == 0:
                above = jnp.where(row > 0, above, 0.0)
            if k == GROUP - 1:
                below = jnp.where(row + GROUP < rows, below, 0.0)
            sources = result[:, k * width : (k + 1) * width].astype(BF16).astype(F32)
            middle_ref[at + k] = advance(
                held[k + 1], held[k], held[k + 2], sources, factors, above, below
            )
        return 0

    lax.fori_loop(0, pieces // GROUP, body, 0, unroll=UNROLL)


def advance(here, above, below, sources, factors, from_above, from_below):
    width = here.shape[1]
    west = pltpu.roll(here, 1, 1)
    east = pltpu.roll(here, width - 1, 1)
    result = factors[0:1] * here + from_above * above + from_below * below
    return result + factors[3:4] * west + factors[4:5] * east + factors[5:6] * sources


def step_kernel(
    rows,
    cells_ref,
    partial_ref,
    top_ref,
    bottom_ref,
    factors_ref,
    in_ref,
    mid_ref,
    bias_ref,
    out_ref,
    change_ref,
    middle,
    scratch,
):
    levels = cells_ref.shape[0] // rows
    kinds, width = cells_ref.shape[1:]
    ahead = rows + 2
    edge = []
    for level in range(levels):
        edge += [top_ref[level * 2 + 1], bottom_ref[level * 2]]
    result = network(
        jnp.concatenate(edge, axis=1), in_ref[...], mid_ref[...], bias_ref[...], out_ref[...]
    ).astype(BF16).astype(F32)
    for level in range(levels):
        base, inside = level * ahead, level * rows
        for k in range(2):
            piece = [top_ref, bottom_ref][k][level * 2 : level * 2 + 2].astype(F32)
            near = cells_ref[inside + k * (rows - 1)].astype(F32)
            at = base + k * (ahead - 1)
            factors = factors_ref[at]
            column = (2 * level + k) * width
            middle[at] = advance(
                piece[1 - k],
                piece[0] if k == 0 else near,
                near if k == 0 else piece[1],
                result[:, column : column + width],
                factors,
                factors[1:2],
                factors[2:3],
            )
            row = base + 1 + k * (rows - 1)
            term = factors_ref[row][1 + k : 2 + k] * piece[1 - k]
            middle[row] = partial_ref[inside + k * (rows - 1)] + term
        for row in range(1, rows - 1):
            middle[base + 1 + row] = partial_ref[inside + row]

    turns = rows // GROUP

    def second_step(i, _):
        level = i // turns
        row = (i - level * turns) * GROUP
        at = level * ahead + row + 1
        held = [middle[at - 1 + k] for k in range(GROUP + 2)]
        cells = jnp.concatenate([held[k + 1].astype(BF16) for k in range(GROUP)], axis=1)
        result = network(cells, in_ref[...], mid_ref[...], bias_ref[...], out_ref[...])
        for k in range(GROUP):
            factors = factors_ref[at + k]
            value = advance(
                held[k + 1],
                held[k],
                held[k + 2],
                result[:, k * width : (k + 1) * width].astype(BF16).astype(F32),
                factors,
                factors[1:2],
                factors[2:3],
            )
            value = value - factors[6:7] * cells_ref[level * rows + row + k].astype(F32)
            for part in range(scratch.shape[0]):
                scratch[part, pl.ds(level * rows * kinds + row + k, kinds, stride=rows), :] = value[
                    :, part * 128 : (part + 1) * 128
                ]
        return 0

    lax.fori_loop(0, levels * turns, second_step, 0, unroll=UNROLL)
    for level in range(levels):
        for part in range(scratch.shape[0]):
            block = scratch[part, level * rows * kinds : (level + 1) * rows * kinds, :]
            change_ref[:, level, :, part * 128 : (part + 1) * 128] = block.reshape(kinds, rows, 128).astype(BF16)


def kernel_call(kernel, outs, scratch, flops, name):
    return pl.pallas_call(
        kernel,
        out_shape=outs,
        scratch_shapes=scratch,
        cost_estimate=pl.CostEstimate(flops=flops, bytes_accessed=4_000_000, transcendentals=0),
        compiler_params=pltpu.CompilerParams(vmem_limit_bytes=48 * 2**20),
        name=name,
    )


def factors_of(east, north, depth, first_level, levels):
    level = first_level + jnp.arange(levels, dtype=jnp.int32)[:, None, None]
    wet = (level.astype(F32) < depth[None]).astype(F32)
    opened = time_step * wet[:, :-1] * wet[:, 1:]
    plus = opened * (jnp.maximum(east[:, :-1], 0.0) + diffusion)
    minus = opened * (jnp.minimum(east[:, :-1], 0.0) - diffusion)
    inner = wet[:, 1:-1]
    flow = jnp.pad(north[:, 1:-1], ((0, 0), (0, 0), (1, 0)))
    sides = jnp.pad(inner, ((0, 0), (0, 0), (1, 1)))
    opened = time_step * sides[..., :-1] * sides[..., 1:]
    right = opened * (jnp.maximum(flow, 0.0) + diffusion)
    left = opened * (jnp.minimum(flow, 0.0) - diffusion)
    own = inner + (minus[:, :-1] - plus[:, 1:]) + (left[..., :-1] - right[..., 1:])
    return jnp.stack(
        [
            own,
            plus[:, :-1],
            -minus[:, 1:],
            right[..., :-1],
            -left[..., 1:],
            time_step * inner,
            inner,
            jnp.zeros_like(inner),
        ],
        axis=2,
    )


def body(
    tracers,
    east_speed,
    north_speed,
    land_mask,
    bottom_level,
    in_weight,
    in_bias,
    mid_weight,
    mid_bias,
    out_weight,
):
    kinds, levels, length, columns = tracers.shape
    tiles, group = lax.axis_size("tile"), lax.axis_size("tracer")
    halves = 2
    stacks = group // halves
    depth_each, rows = levels // stacks, length // halves
    own = lax.axis_index("tracer")
    half, stack = own // stacks, own % stacks
    all_kinds = kinds * group
    pieces = depth_each * rows

    sent = tracers.astype(BF16).reshape(kinds, stacks, depth_each, halves, rows, columns)
    sent = sent.transpose(3, 1, 0, 2, 4, 5).reshape(group, kinds, depth_each, rows, columns)
    cells = lax.all_to_all(sent, "tracer", split_axis=0, concat_axis=0, tiled=True)
    cells = cells.reshape(all_kinds, depth_each, rows, columns)

    east_speed, north_speed, land_mask, sent = lax.optimization_barrier(
        (east_speed, north_speed, land_mask, sent)
    )
    depth = jnp.where(land_mask == 1, bottom_level, 0).astype(F32)
    first_level = stack * depth_each
    east = lax.dynamic_slice_in_dim(east_speed, first_level, depth_each, 0)
    north = lax.dynamic_slice_in_dim(north_speed, first_level, depth_each, 0)
    geometry = jnp.concatenate([east, north, depth[None]], axis=0)

    def at(tile, part, place):
        return tile * group + part * stacks + place

    across, back, within = [], [], []
    for place in range(stacks):
        for tile in range(tiles):
            within.append((at(tile, 0, place), at(tile, 1, place)))
            if tile + 1 < tiles:
                across.append((at(tile, 1, place), at(tile + 1, 0, place)))
    back = [(j, i) for i, j in across]
    axes = ("tile", "tracer")
    edge = lax.dynamic_slice_in_dim(geometry, half * (length - 2), 2, 1)
    arrived = lax.ppermute(edge, axes, across + back)
    geometry = jnp.where(
        half == 0,
        jnp.concatenate([arrived, geometry[:, : rows + 2]], axis=1),
        jnp.concatenate([geometry[:, rows - 2 :], arrived], axis=1),
    )
    factors = factors_of(
        geometry[:depth_each],
        geometry[depth_each : 2 * depth_each],
        geometry[2 * depth_each],
        first_level,
        depth_each,
    ).reshape(depth_each * (rows + 2), 8, columns)

    def parts(value):
        high = value.astype(BF16)
        low = (value - high.astype(F32)).astype(BF16)
        return [high, low, (value - high.astype(F32) - low.astype(F32)).astype(BF16)]

    in_parts = jnp.stack(parts(0.5 * in_bias) + [jnp.zeros(in_bias.shape, BF16)] * 13, axis=1)
    weights = (
        jnp.concatenate([(0.5 * in_weight.astype(F32)).astype(BF16).T, in_parts], axis=1),
        (0.5 * mid_weight.astype(F32)).astype(BF16).T,
        jnp.broadcast_to(0.5 * mid_bias[:, None], mid_bias.shape + (128,)),
        out_weight.T,
    )

    hidden = in_weight.shape[1]
    per_piece = 2 * columns * hidden * (hidden + 2 * all_kinds)
    turned, first, last = kernel_call(
        functools.partial(turn_kernel, rows),
        [
            jax.ShapeDtypeStruct((pieces, all_kinds, columns), BF16),
            jax.ShapeDtypeStruct((depth_each * 2, all_kinds, columns), BF16),
            jax.ShapeDtypeStruct((depth_each * 2, all_kinds, columns), BF16),
        ],
        [pltpu.VMEM((columns // 128, all_kinds * rows, 128), F32)],
        1_000_000,
        "turn",
    )(cells)
    top = lax.ppermute(last, axes, within + across)
    bottom = lax.ppermute(first, axes, [(j, i) for i, j in within] + back)
    partial = kernel_call(
        functools.partial(source_kernel, rows),
        jax.ShapeDtypeStruct(turned.shape, F32),
        [],
        pieces * per_piece,
        "sources",
    )(turned, factors, *weights)
    change = kernel_call(
        functools.partial(step_kernel, rows),
        jax.ShapeDtypeStruct(cells.shape, BF16),
        [
            pltpu.VMEM((depth_each * (rows + 2), all_kinds, columns), F32),
            pltpu.VMEM((columns // 128, depth_each * rows * all_kinds, 128), F32),
        ],
        pieces * per_piece,
        "steps",
    )(turned, partial, top, bottom, factors, *weights)

    change = change.reshape(group, kinds, depth_each, rows, columns)
    change = lax.all_to_all(change, "tracer", split_axis=0, concat_axis=0, tiled=True)
    change = change.reshape(halves, stacks, kinds, depth_each, rows, columns)
    change = change.transpose(2, 1, 3, 0, 4, 5).reshape(kinds, levels, length, columns)
    level = jnp.arange(levels, dtype=jnp.int32)[:, None, None]
    wet = (level.astype(F32) < depth[None]).astype(F32)
    return wet[None] * (tracers + change.astype(F32))


def solution(mesh):
    return jax.shard_map(
        body,
        mesh=mesh,
        in_specs=(
            P("tracer", None, "tile", None),
            P(None, "tile", None),
            P(None, "tile", None),
            P("tile", None),
            P("tile", None),
            P(),
            P(),
            P(),
            P(),
            P(),
        ),
        out_specs=P("tracer", None, "tile", None),
        check_vma=False,
    )
```

```python
import functools
import math

import jax
import jax.numpy as jnp
from jax import lax
from jax.experimental import pallas as pl
from jax.experimental.pallas import tpu as pltpu
from jax.sharding import PartitionSpec as P

STEPS = 2
diffusion = 0.2
time_step = 0.2
GROUP = 4

BF16 = jnp.bfloat16
F32 = jnp.float32


def silu_of_half(half):
    return (half + half * jnp.tanh(half)).astype(BF16)


def network(cells, in_weight, mid_weight, mid_bias, out_weight):
    lanes = cells.shape[1]
    cells = jnp.concatenate([cells, jnp.ones((16, lanes), BF16)], axis=0)
    hidden = silu_of_half(jnp.dot(in_weight, cells, preferred_element_type=F32))
    hidden = jnp.dot(mid_weight, hidden, preferred_element_type=F32)
    hidden = silu_of_half(hidden + jnp.concatenate([mid_bias] * (lanes // 128), axis=1))
    return jnp.dot(out_weight, hidden, preferred_element_type=F32)


def turn_kernel(rows, x_ref, turned_ref, first_ref, last_ref, scratch):
    kinds, levels = x_ref.shape[:2]
    for level in range(levels):
        for part in range(scratch.shape[0]):
            block = x_ref[:, level, :, part * 128 : (part + 1) * 128]
            scratch[part] = block.astype(F32).reshape(kinds * rows, 128)
        for row in range(rows):
            picked = [scratch[part, pl.ds(row, kinds, stride=rows), :] for part in range(scratch.shape[0])]
            piece = jnp.concatenate(picked, axis=1).astype(BF16)
            turned_ref[level * rows + row] = piece
            if row < 2:
                first_ref[level * 2 + row] = piece
            if row >= rows - 2:
                last_ref[level * 2 + row - rows + 2] = piece


def advance(here, above, below, sources, factors, from_above, from_below):
    width = here.shape[1]
    west = pltpu.roll(here, 1, 1)
    east = pltpu.roll(here, width - 1, 1)
    result = factors[0:1] * here + from_above * above + from_below * below
    return result + factors[3:4] * west + factors[4:5] * east + factors[5:6] * sources


def nt(rows, table):
    return lax.dot_general(rows, table, (((1,), (1,)), ((), ())), preferred_element_type=F32)


def nn(rows, table):
    return jnp.dot(rows, table, preferred_element_type=F32)


def one_hot(place):
    width = place.shape[1]
    slots = lax.broadcasted_iota(jnp.int32, (width, width), 0).astype(F32)
    return jnp.where(slots == place, 1.0, 0.0).astype(BF16)


def halves_of(ref, start, size, stride):
    return jnp.concatenate(
        [ref[part, pl.ds(start, size, stride=stride), :] for part in range(ref.shape[0])], axis=1
    )


def put_halves(ref, start, size, stride, value):
    for part in range(ref.shape[0]):
        ref[part, pl.ds(start, size, stride=stride), :] = value[:, part * 128 : (part + 1) * 128]


def pack_kernel(x_ref, land_ref, bottom_ref, sent_ref, place_ref, depth_ref, counts, table, held, packed):
    kinds, levels, length, width = x_ref.shape
    halves, stacks, _, _, rows, _ = sent_ref.shape
    depth_ref[...] = jnp.where(land_ref[...] == 1, bottom_ref[...], 0).astype(F32)
    bins = 32
    value = lax.broadcasted_iota(jnp.int32, (bins, width), 0).astype(F32)
    for row in range(length):
        depth = depth_ref[row : row + 1]
        counts[row * bins : (row + 1) * bins, :width] = jnp.where(depth == value, 1.0, 0.0).astype(BF16)
        counts[row * bins : (row + 1) * bins, width:] = jnp.where(depth > value, 1.0, 0.0).astype(BF16)
    before = lax.broadcasted_iota(jnp.int32, (width, width), 0)
    after = lax.broadcasted_iota(jnp.int32, (width, width), 1)
    table[:width] = jnp.where(before < after, 1.0, 0.0).astype(BF16)
    table[width:] = jnp.ones((width, width), BF16)
    ranks = nn(counts[...], table[...])
    for row in range(length):
        here = jnp.where(depth_ref[row : row + 1] == value, ranks[row * bins : (row + 1) * bins], 0.0)
        place = jnp.sum(here, axis=0, keepdims=True)
        place_ref[row : row + 1] = place if row % 2 == 0 else (width - 1.0) - place

    thin = levels - stacks
    for kind in range(kinds):
        for part in range(held.shape[0]):
            block = x_ref[kind, stacks:, :, part * 128 : (part + 1) * 128]
            held[part, kind * thin * length : (kind + 1) * thin * length] = block.reshape(thin * length, 128)
    level = stacks + lax.broadcasted_iota(jnp.int32, (thin, width), 0).astype(F32)

    def body(i, _):
        sorted_rows = []
        for k in range(2):
            row = 2 * i + k
            wet = level < depth_ref[pl.ds(row, 1)]
            cells = [
                jnp.where(wet, halves_of(held, kind * thin * length + row, thin, length), 0.0).astype(BF16)
                for kind in range(kinds)
            ]
            sorted_rows.append(nt(jnp.concatenate(cells, axis=0), one_hot(place_ref[pl.ds(row, 1)])))
        for k in range(2):
            for kind in range(kinds):
                at = kind * thin
                deep = sorted_rows[1 - k][at + stacks : at + 2 * stacks]
                value = sorted_rows[k][at : at + stacks] + pltpu.roll(deep, stacks // 2, 0)
                put_halves(packed, kind * stacks * length + 2 * i + k, stacks, length, value)
        return 0

    lax.fori_loop(0, length // 2, body, 0, unroll=2)
    for half in range(halves):
        inside = slice(half * rows, (half + 1) * rows)
        for kind in range(kinds):
            sent_ref[half, :, kind, 0] = x_ref[kind, :stacks, inside].astype(BF16)
            for part in range(packed.shape[0]):
                at = kind * stacks * length
                block = packed[part, at : at + stacks * length].reshape(stacks, length, 128)
                sent_ref[half, :, kind, 1, :, part * 128 : (part + 1) * 128] = block[:, inside].astype(BF16)


def finish_kernel(x_ref, arrived_ref, place_ref, land_ref, bottom_ref, result_ref, held, spread):
    kinds, levels, length, width = x_ref.shape
    halves, stacks, _, _, rows, _ = arrived_ref.shape
    thin = levels - stacks
    each = stacks * kinds * rows
    for half in range(halves):
        for part in range(held.shape[0]):
            block = arrived_ref[half, :, :, 1, :, part * 128 : (part + 1) * 128]
            held[part, half * each : (half + 1) * each] = block.astype(F32).reshape(each, 128)

    def body(i, _):
        half = i // (rows // 2)
        row = 2 * i - half * rows
        cells = []
        for k in range(2):
            for kind in range(kinds):
                cells.append(halves_of(held, half * each + kind * rows + row + k, stacks, kinds * rows))
        cells = jnp.concatenate(cells, axis=0).astype(BF16)
        for k in range(2):
            value = nn(cells, one_hot(place_ref[pl.ds(2 * i + k, 1)]))
            for kind in range(kinds):
                near = (k * kinds + kind) * stacks
                other = ((1 - k) * kinds + kind) * stacks
                at = kind * thin * length + 2 * i + k
                put_halves(spread, at, stacks, length, value[near : near + stacks])
                deep = pltpu.roll(value[other : other + stacks], stacks // 2, 0)
                put_halves(spread, at + stacks * length, stacks, length, deep)
        return 0

    lax.fori_loop(0, length // 2, body, 0, unroll=2)
    depth = jnp.where(land_ref[...] == 1, bottom_ref[...], 0)
    for kind in range(kinds):
        for level in range(levels):
            if level < stacks:
                change = jnp.concatenate(
                    [arrived_ref[half, level, kind, 0] for half in range(halves)], axis=0
                ).astype(F32)
            else:
                at = (kind * thin + level - stacks) * length
                change = jnp.concatenate(
                    [spread[part, at : at + length] for part in range(spread.shape[0])], axis=1
                )
            result_ref[kind, level] = jnp.where(level < depth, x_ref[kind, level] + change, 0.0)


def source_kernel(
    rows, cells_ref, table_ref, factors_ref, in_ref, mid_ref, bias_ref, out_ref, middle_ref, spread_ref, held
):
    _, kinds, width = cells_ref.shape
    ahead = rows + 2
    weights = (in_ref, mid_ref, bias_ref, out_ref)

    def cell(level, row):
        if level == 0:
            return cells_ref[row]
        return spread_ref[(level - 1) * rows + row]

    def spread_out(i, _):
        row = 2 * i
        cells = jnp.concatenate([cells_ref[rows + row], cells_ref[rows + row + 1]], axis=0)
        for k in range(2):
            value = nn(cells, table_ref[row + 2 + k]).astype(BF16)
            spread_ref[row + k] = value[k * kinds : (k + 1) * kinds]
            spread_ref[rows + row + k] = value[(1 - k) * kinds : (2 - k) * kinds]
        return 0

    lax.fori_loop(0, rows // 2, spread_out, 0, unroll=2)

    def sources(i):
        row = 2 * i
        cells = [cells_ref[row], cells_ref[row + 1], cells_ref[rows + row], cells_ref[rows + row + 1]]
        result = network(jnp.concatenate(cells, axis=1), *[ref[...] for ref in weights])
        held[i] = result.astype(BF16)

    def move(i):
        row = 2 * i
        result = held[i]
        packed = jnp.concatenate(
            [result[:, 2 * width : 3 * width], result[:, 3 * width :]], axis=0
        )
        for k in range(2):
            value = nn(packed, table_ref[row + 2 + k])
            pieces = [
                result[:, k * width : (k + 1) * width].astype(F32),
                value[k * kinds : (k + 1) * kinds],
                value[(1 - k) * kinds : (2 - k) * kinds],
            ]
            for level in range(3):
                factors = factors_ref[level * ahead + row + 1 + k]
                above, below = factors[1:2], factors[2:3]
                if k == 0:
                    above = jnp.where(row > 0, above, 0.0)
                else:
                    below = jnp.where(row + 2 < rows, below, 0.0)
                middle_ref[level * rows + row + k] = advance(
                    cell(level, row + k).astype(F32),
                    cell(level, jnp.maximum(row + k - 1, 0)).astype(F32),
                    cell(level, jnp.minimum(row + k + 1, rows - 1)).astype(F32),
                    pieces[level],
                    factors,
                    above,
                    below,
                )

    def body(i, _):
        move(i - 1)
        sources(i)
        return 0

    sources(0)
    lax.fori_loop(1, rows // 2, body, 0)
    move(rows // 2 - 1)


def step_kernel(
    rows,
    cells_ref,
    spread_ref,
    partial_ref,
    top_ref,
    bottom_ref,
    table_ref,
    factors_ref,
    in_ref,
    mid_ref,
    bias_ref,
    out_ref,
    change_ref,
    middle,
    packed,
    held,
    scratch,
):
    _, kinds, width = cells_ref.shape
    ahead = rows + 2
    weights = (in_ref, mid_ref, bias_ref, out_ref)

    def run(cells):
        return network(jnp.concatenate(cells, axis=1), *[ref[...] for ref in weights]).astype(BF16)

    edges = [
        [top_ref[1], top_ref[2], top_ref[3]],
        [bottom_ref[0], bottom_ref[2], bottom_ref[3]],
    ]
    result = run(edges[0] + edges[1])
    for k in range(2):
        packed_cells = jnp.concatenate(edges[k][1:], axis=0)
        at = 3 * k * width
        packed_sources = jnp.concatenate(
            [result[:, at + width : at + 2 * width], result[:, at + 2 * width : at + 3 * width]], axis=0
        )
        near = nn(jnp.concatenate([packed_cells, packed_sources], axis=0), table_ref[[1, rows + 2][k]])
        far = nn(packed_cells, table_ref[[0, rows + 3][k]])
        near_at = [[1, 0], [0, 1]][k]
        far_at = [[0, 1], [1, 0]][k]
        for level in range(3):
            inside = level * rows + k * (rows - 1)
            if level == 0:
                own = edges[k][0].astype(F32)
                other = (top_ref[0] if k == 0 else bottom_ref[1]).astype(F32)
                sources = result[:, at : at + width].astype(F32)
                inner = cells_ref[k * (rows - 1)].astype(F32)
            else:
                place = near_at[level - 1] * kinds
                own = near[place : place + kinds]
                sources = near[2 * kinds + place : 3 * kinds + place]
                place = far_at[level - 1] * kinds
                other = far[place : place + kinds]
                inner = spread_ref[(level - 1) * rows + k * (rows - 1)].astype(F32)
            row = level * ahead + k * (ahead - 1)
            factors = factors_ref[row]
            middle[row] = advance(
                own,
                other if k == 0 else inner,
                inner if k == 0 else other,
                sources,
                factors,
                factors[1:2],
                factors[2:3],
            )
            row = level * ahead + 1 + k * (rows - 1)
            middle[row] = partial_ref[inside] + factors_ref[row][1 + k : 2 + k] * own
    for level in range(3):
        for row in range(1, rows - 1):
            middle[level * ahead + 1 + row] = partial_ref[level * rows + row]

    def put_together(row, thin):
        values = [nt(thin[k], table_ref[row + 2 + k]) for k in range(2)]
        return [values[k][:kinds] + values[1 - k][kinds:] for k in range(2)]

    def pack(i, _):
        row = 2 * i
        thin = [
            jnp.concatenate(
                [middle[level * ahead + 1 + row + k].astype(BF16) for level in (1, 2)], axis=0
            )
            for k in range(2)
        ]
        values = put_together(row, thin)
        for k in range(2):
            packed[row + k] = values[k].astype(BF16)
        return 0

    lax.fori_loop(0, rows // 2, pack, 0, unroll=2)

    def sources_of(i):
        row = 2 * i
        cells = [middle[1 + row + k].astype(BF16) for k in range(2)]
        held[i] = run(cells + [packed[row], packed[row + 1]])

    def move(i):
        row = 2 * i
        result = held[i]
        thin_sources = jnp.concatenate(
            [result[:, 2 * width : 3 * width], result[:, 3 * width :]], axis=0
        )
        changes = []
        for k in range(2):
            value = nn(thin_sources, table_ref[row + 2 + k])
            pieces = [
                result[:, k * width : (k + 1) * width].astype(F32),
                value[k * kinds : (k + 1) * kinds],
                value[(1 - k) * kinds : (2 - k) * kinds],
            ]
            for level in range(3):
                at = level * ahead + 1 + row + k
                factors = factors_ref[at]
                value = advance(
                    middle[at],
                    middle[at - 1],
                    middle[at + 1],
                    pieces[level],
                    factors,
                    factors[1:2],
                    factors[2:3],
                )
                if level == 0:
                    first = cells_ref[row + k]
                else:
                    first = spread_ref[(level - 1) * rows + row + k]
                changes.append(value - factors[6:7] * first.astype(F32))
        thin = [
            jnp.concatenate([changes[3 * k + 1].astype(BF16), changes[3 * k + 2].astype(BF16)], axis=0)
            for k in range(2)
        ]
        values = put_together(row, thin)
        for k in range(2):
            put_halves(scratch, row + k, kinds, rows, changes[3 * k])
            put_halves(scratch, rows * kinds + row + k, kinds, rows, values[k])

    def body(i, _):
        move(i - 1)
        sources_of(i)
        return 0

    sources_of(0)
    lax.fori_loop(1, rows // 2, body, 0)
    move(rows // 2 - 1)
    for level in range(2):
        for part in range(scratch.shape[0]):
            block = scratch[part, level * rows * kinds : (level + 1) * rows * kinds, :]
            change_ref[:, level, :, part * 128 : (part + 1) * 128] = block.reshape(kinds, rows, 128).astype(BF16)


def kernel_call(kernel, outs, scratch, flops, name):
    return pl.pallas_call(
        kernel,
        out_shape=outs,
        scratch_shapes=scratch,
        cost_estimate=pl.CostEstimate(flops=flops, bytes_accessed=4_000_000, transcendentals=0),
        compiler_params=pltpu.CompilerParams(vmem_limit_bytes=24 * 2**20),
        name=name,
    )


def factors_of(east, north, depth, level):
    wet = (level[:, None, None] < depth[None]).astype(F32)
    opened = time_step * wet[:, :-1] * wet[:, 1:]
    plus = opened * (jnp.maximum(east[:, :-1], 0.0) + diffusion)
    minus = opened * (jnp.minimum(east[:, :-1], 0.0) - diffusion)
    inner = wet[:, 1:-1]
    flow = jnp.pad(north[:, 1:-1], ((0, 0), (0, 0), (1, 0)))
    sides = jnp.pad(inner, ((0, 0), (0, 0), (1, 1)))
    opened = time_step * sides[..., :-1] * sides[..., 1:]
    right = opened * (jnp.maximum(flow, 0.0) + diffusion)
    left = opened * (jnp.minimum(flow, 0.0) - diffusion)
    own = inner + (minus[:, :-1] - plus[:, 1:]) + (left[..., :-1] - right[..., 1:])
    return jnp.stack(
        [
            own,
            plus[:, :-1],
            -minus[:, 1:],
            right[..., :-1],
            -left[..., 1:],
            time_step * inner,
            inner,
            jnp.zeros_like(inner),
        ],
        axis=2,
    )


def with_halo(value, sides, width):
    for axis, dim in sides:
        size, length = (lax.axis_size(axis), value.shape[dim])
        up = [(i, (i + 1) % size) for i in range(size - 1)]
        down = [(j, i) for i, j in up]
        last = lax.slice_in_dim(value, length - width, length, axis=dim)
        initial = lax.slice_in_dim(value, 0, width, axis=dim)
        before = lax.ppermute(last, axis, up)
        after = lax.ppermute(initial, axis, down)
        value = jnp.concatenate([before, value, after], axis=dim)
    return value


def as_sent(value):
    return jax.tree.map(lambda a: a.astype(jnp.bfloat16) if a.dtype == jnp.float32 else a, value)


def face_flux(behind_cells, ahead_cells, flow_speed, opened):
    moved = jnp.maximum(flow_speed, 0.0) * behind_cells + jnp.minimum(flow_speed, 0.0) * ahead_cells
    return opened * (moved - diffusion * (ahead_cells - behind_cells))


def plain_network(inputs, in_weight, in_bias, mid_weight, mid_bias, out_weight):
    kinds, depth, rows, cols = inputs.shape
    cells = depth * rows * cols
    turns = math.gcd(cells, 8)
    blocked = jnp.moveaxis(inputs.reshape(kinds, turns, cells // turns), 1, 0)

    def one_block(cell_block):
        first_hidden = (
            jnp.einsum("tn,th->nh", cell_block, in_weight, preferred_element_type=jnp.float32)
            + in_bias
        )
        first_hidden = jax.nn.silu(first_hidden).astype(jnp.bfloat16)
        second_hidden = (
            jnp.einsum("nh,hk->nk", first_hidden, mid_weight, preferred_element_type=jnp.float32)
            + mid_bias
        )
        second_hidden = jax.nn.silu(second_hidden).astype(jnp.bfloat16)
        return jnp.einsum(
            "nh,ht->tn", second_hidden, out_weight, preferred_element_type=jnp.float32
        ).astype(jnp.bfloat16)

    result = jnp.moveaxis(lax.map(one_block, blocked), 0, 1)
    return result.reshape(result.shape[0], depth, rows, cols)


def plain_body(
    tracers,
    east_speed,
    north_speed,
    land_mask,
    bottom_level,
    in_weight,
    in_bias,
    mid_weight,
    mid_bias,
    out_weight,
):
    levels = east_speed.shape[0]
    depth = jnp.arange(levels, dtype=jnp.int32)[:, None, None]
    wet_cells = ((land_mask[None] == 1) & (depth < bottom_level[None])).astype(jnp.float32)
    geometry = with_halo(
        jnp.stack([east_speed, wet_cells]).astype(jnp.bfloat16), (("tile", 2),), 1
    ).astype(jnp.float32)
    flow_x = geometry[0, :, :-1]
    wet_x = geometry[1]
    opened_x = wet_x[:, :-1] * wet_x[:, 1:]
    flow_y = jnp.pad(north_speed, ((0, 0), (0, 0), (1, 0)))
    wet_y = jnp.pad(wet_cells, ((0, 0), (0, 0), (1, 1)))
    opened_y = wet_y[..., :-1] * wet_y[..., 1:]
    field = tracers
    for step in range(STEPS):
        padded = with_halo(as_sent(field), (("tile", 2),), 1).astype(field.dtype)
        inputs = field.astype(jnp.bfloat16)
        local_sources = plain_network(
            lax.all_to_all(inputs, "tracer", split_axis=2, concat_axis=0, tiled=True),
            in_weight,
            in_bias,
            mid_weight,
            mid_bias,
            out_weight,
        )
        sources = lax.all_to_all(local_sources, "tracer", split_axis=0, concat_axis=2, tiled=True)
        x_flux = face_flux(padded[:, :, :-1], padded[:, :, 1:], flow_x, opened_x)
        cells_y = jnp.pad(field, ((0, 0), (0, 0), (0, 0), (1, 1)))
        y_flux = face_flux(cells_y[..., :-1], cells_y[..., 1:], flow_y, opened_y)
        tendency = x_flux[:, :, :-1] - x_flux[:, :, 1:] + (y_flux[..., :-1] - y_flux[..., 1:])
        field = wet_cells[None] * (field + time_step * (tendency + sources.astype(jnp.float32)))
    return field


def split_parts(value, count):
    parts = []
    for _ in range(count):
        parts.append(value.astype(BF16))
        value = value - parts[-1].astype(F32)
    return parts


def body(
    tracers,
    east_speed,
    north_speed,
    land_mask,
    bottom_level,
    in_weight,
    in_bias,
    mid_weight,
    mid_bias,
    out_weight,
):
    arguments = (
        tracers,
        east_speed,
        north_speed,
        land_mask,
        bottom_level,
        in_weight,
        in_bias,
        mid_weight,
        mid_bias,
        out_weight,
    )
    kinds, levels, length, columns = tracers.shape
    tiles, group = lax.axis_size("tile"), lax.axis_size("tracer")
    halves = 2
    stacks = group // halves
    rows = length // halves
    own = lax.axis_index("tracer")
    half, stack = own // stacks, own % stacks
    all_kinds = kinds * group
    thin = levels - stacks
    parts = columns // 128

    sent, place = kernel_call(
        pack_kernel,
        [
            jax.ShapeDtypeStruct((halves, stacks, kinds, 2, rows, columns), BF16),
            jax.ShapeDtypeStruct((length, columns), F32),
        ],
        [
            pltpu.VMEM((length, columns), F32),
            pltpu.VMEM((length * 32, 2 * columns), BF16),
            pltpu.VMEM((2 * columns, columns), BF16),
            pltpu.VMEM((parts, kinds * thin * length, 128), F32),
            pltpu.VMEM((parts, kinds * stacks * length, 128), F32),
        ],
        2 * length * columns * columns * (32 + 64),
        "pack",
    )(tracers, land_mask, bottom_level)
    sent = sent.reshape(group, kinds, 2, rows, columns)
    cells = lax.all_to_all(sent, "tracer", split_axis=0, concat_axis=0, tiled=True)
    cells = cells.reshape(all_kinds, 2, rows, columns)

    east_speed, north_speed, land_mask, sent = lax.optimization_barrier(
        (east_speed, north_speed, land_mask, sent)
    )
    depth = jnp.where(land_mask == 1, bottom_level, 0).astype(F32)
    level_list = [stack, stacks + stack, 2 * stacks + (stack + stacks // 2) % stacks]

    side, position = stack // (stacks // 2), stack % (stacks // 2)

    def own_levels(value):
        value = value.reshape(2 * levels // stacks, stacks // 2, length, columns)
        value = lax.dynamic_slice_in_dim(value, position, 1, 1)[:, 0]
        return jnp.where(
            side == 0,
            jnp.stack([value[0], value[2], value[5]]),
            jnp.stack([value[1], value[3], value[4]]),
        )

    geometry = [own_levels(east_speed), own_levels(north_speed), depth[None], place[None]]

    def at(tile, part, position):
        return tile * group + part * stacks + position

    across, within = [], []
    for position in range(stacks):
        for tile in range(tiles):
            within.append((at(tile, 0, position), at(tile, 1, position)))
            if tile + 1 < tiles:
                across.append((at(tile, 1, position), at(tile + 1, 0, position)))
    back = [(j, i) for i, j in across]
    axes = ("tile", "tracer")
    edge = jnp.concatenate(
        [lax.dynamic_slice_in_dim(value, half * (length - 2), 2, 1) for value in geometry], axis=0
    )
    arrived = lax.ppermute(edge, axes, across + back)
    arrived = [arrived[:3], arrived[3:6], arrived[6:7], arrived[7:8]]

    def widened(value, outside):
        return jnp.where(
            half == 0,
            jnp.concatenate([outside, value[:, : rows + 2]], axis=1),
            jnp.concatenate([value[:, rows - 2 :], outside], axis=1),
        )

    east, north, wide_depth, wide_place = [widened(*pair) for pair in zip(geometry, arrived)]
    factors = factors_of(east, north, wide_depth[0], jnp.stack(level_list).astype(F32)).reshape(
        3 * (rows + 2), 8, columns
    )
    slots = jnp.arange(columns, dtype=jnp.int32).astype(F32)
    table = (slots[None, :, None] == wide_place[0][:, None, :]).astype(BF16)

    in_parts = jnp.stack(split_parts(0.5 * in_bias, 3) + [jnp.zeros(in_bias.shape, BF16)] * 13, axis=1)
    weights = (
        jnp.concatenate([(0.5 * in_weight.astype(F32)).astype(BF16).T, in_parts], axis=1),
        (0.5 * mid_weight.astype(F32)).astype(BF16).T,
        jnp.broadcast_to(0.5 * mid_bias[:, None], mid_bias.shape + (128,)),
        out_weight.T,
    )

    hidden = in_weight.shape[1]
    pieces = 2 * rows
    per_piece = 2 * columns * hidden * (hidden + 2 * all_kinds)
    turned, first, last = kernel_call(
        functools.partial(turn_kernel, rows),
        [
            jax.ShapeDtypeStruct((pieces, all_kinds, columns), BF16),
            jax.ShapeDtypeStruct((4, all_kinds, columns), BF16),
            jax.ShapeDtypeStruct((4, all_kinds, columns), BF16),
        ],
        [pltpu.VMEM((parts, all_kinds * rows, 128), F32)],
        1_000_000,
        "turn",
    )(cells)
    top = lax.ppermute(last, axes, within + across)
    bottom = lax.ppermute(first, axes, [(j, i) for i, j in within] + back)
    partial, spread = kernel_call(
        functools.partial(source_kernel, rows),
        [
            jax.ShapeDtypeStruct((3 * rows, all_kinds, columns), F32),
            jax.ShapeDtypeStruct((2 * rows, all_kinds, columns), BF16),
        ],
        [pltpu.VMEM((rows // 2, all_kinds, 4 * columns), BF16)],
        pieces * per_piece,
        "sources",
    )(turned, table, factors, *weights)
    change = kernel_call(
        functools.partial(step_kernel, rows),
        jax.ShapeDtypeStruct(cells.shape, BF16),
        [
            pltpu.VMEM((3 * (rows + 2), all_kinds, columns), F32),
            pltpu.VMEM((rows, all_kinds, columns), BF16),
            pltpu.VMEM((rows // 2, all_kinds, 4 * columns), BF16),
            pltpu.VMEM((parts, 2 * rows * all_kinds, 128), F32),
        ],
        pieces * per_piece,
        "steps",
    )(turned, spread, partial, top, bottom, table, factors, *weights)

    depth, change = lax.optimization_barrier((depth, change))
    level = jnp.arange(levels, dtype=jnp.int32).astype(F32)
    count = jnp.sum((level[:, None, None] < depth[None]).astype(F32), axis=2)
    deep = jnp.roll(count[2 * stacks :], -(stacks // 2), axis=0)
    deep = jnp.flip(deep.reshape(stacks, length // 2, 2), axis=2).reshape(stacks, length)
    fullest = jnp.full((8, 128), jnp.max(count[stacks : 2 * stacks] + deep))
    step = 1
    while step < tiles:
        pairs = [(tile, tile ^ step) for tile in range(tiles)]
        fullest = jnp.maximum(fullest, lax.ppermute(fullest, "tile", pairs))
        step *= 2
    excess = fullest[0, 0] > columns

    change = change.reshape(group, kinds, 2, rows, columns)
    change = lax.all_to_all(change, "tracer", split_axis=0, concat_axis=0, tiled=True)
    change = change.reshape(halves, stacks, kinds, 2, rows, columns)

    def finish(change, place, arguments):
        return kernel_call(
            finish_kernel,
            jax.ShapeDtypeStruct(tracers.shape, F32),
            [
                pltpu.VMEM((parts, group * kinds * rows, 128), F32),
                pltpu.VMEM((parts, kinds * thin * length, 128), F32),
            ],
            2 * length * columns * columns * 32,
            "finish",
        )(arguments[0], change, place, arguments[3], arguments[4])

    def in_full(change, place, arguments):
        return plain_body(*arguments)

    return lax.cond(excess, in_full, finish, change, place, arguments)


def solution(mesh):
    return jax.shard_map(
        body,
        mesh=mesh,
        in_specs=(
            P("tracer", None, "tile", None),
            P(None, "tile", None),
            P(None, "tile", None),
            P("tile", None),
            P("tile", None),
            P(),
            P(),
            P(),
            P(),
            P(),
        ),
        out_specs=P("tracer", None, "tile", None),
        check_vma=False,
    )
```

```python
import functools
import math

import jax
import jax.numpy as jnp
from jax import lax
from jax.experimental import pallas as pl
from jax.experimental.pallas import tpu as pltpu
from jax.sharding import PartitionSpec as P

STEPS = 2
diffusion = 0.2
time_step = 0.2
GROUP = 4

BF16 = jnp.bfloat16
F32 = jnp.float32


def silu_of_half(half):
    return (half + half * jnp.tanh(half)).astype(BF16)


def network(cells, in_weight, mid_weight, mid_bias, out_weight):
    lanes = cells.shape[1]
    cells = jnp.concatenate([cells, jnp.ones((16, lanes), BF16)], axis=0)
    hidden = silu_of_half(jnp.dot(in_weight, cells, preferred_element_type=F32))
    hidden = jnp.dot(mid_weight, hidden, preferred_element_type=F32)
    hidden = silu_of_half(hidden + jnp.concatenate([mid_bias] * (lanes // 128), axis=1))
    return jnp.dot(out_weight, hidden, preferred_element_type=F32)


def turn_kernel(rows, x_ref, turned_ref, first_ref, last_ref, scratch):
    kinds, levels = x_ref.shape[:2]
    for level in range(levels):
        for part in range(scratch.shape[0]):
            block = x_ref[:, level, :, part * 128 : (part + 1) * 128]
            scratch[part] = block.astype(F32).reshape(kinds * rows, 128)
        for row in range(rows):
            picked = [scratch[part, pl.ds(row, kinds, stride=rows), :] for part in range(scratch.shape[0])]
            piece = jnp.concatenate(picked, axis=1).astype(BF16)
            turned_ref[level * rows + row] = piece
            if row < 2:
                first_ref[level * 2 + row] = piece
            if row >= rows - 2:
                last_ref[level * 2 + row - rows + 2] = piece


def advance(here, above, below, sources, factors, from_above, from_below):
    width = here.shape[1]
    west = pltpu.roll(here, 1, 1)
    east = pltpu.roll(here, width - 1, 1)
    result = factors[0:1] * here + from_above * above + from_below * below
    return result + factors[3:4] * west + factors[4:5] * east + factors[5:6] * sources


def nt(rows, table):
    return lax.dot_general(rows, table, (((1,), (1,)), ((), ())), preferred_element_type=F32)


def nn(rows, table):
    return jnp.dot(rows, table, preferred_element_type=F32)


def one_hot(place):
    width = place.shape[1]
    slots = lax.broadcasted_iota(jnp.int32, (width, width), 0).astype(F32)
    return jnp.where(slots == place, 1.0, 0.0).astype(BF16)


def halves_of(ref, start, size, stride):
    return jnp.concatenate(
        [ref[part, pl.ds(start, size, stride=stride), :] for part in range(ref.shape[0])], axis=1
    )


def put_halves(ref, start, size, stride, value):
    for part in range(ref.shape[0]):
        ref[part, pl.ds(start, size, stride=stride), :] = value[:, part * 128 : (part + 1) * 128]


def pack_kernel(
    x_ref, land_ref, bottom_ref, sent_ref, place_ref, depth_ref, counts, table, held, plain, packed, arrivals
):
    kinds, _, width = x_ref.shape
    length = land_ref.shape[0]
    halves, stacks, _, _, rows, _ = sent_ref.shape
    levels = x_ref.shape[1] // length
    thin = levels - stacks
    parts = held.shape[0]
    copies = []
    for kind in range(kinds):
        for part in range(parts):
            copies.append(
                pltpu.make_async_copy(
                    x_ref.at[kind, pl.ds(stacks * length, thin * length), pl.ds(part * 128, 128)],
                    held.at[part, pl.ds(kind * thin * length, thin * length)],
                    arrivals.at[len(copies)],
                )
            )
    copies.append(
        pltpu.make_async_copy(x_ref.at[:, pl.ds(0, stacks * length)], plain, arrivals.at[len(copies)])
    )
    for copy in copies:
        copy.start()
    depth_ref[...] = jnp.where(land_ref[...] == 1, bottom_ref[...], 0).astype(F32)
    bins = 32
    value = lax.broadcasted_iota(jnp.int32, (bins, width), 0).astype(F32)
    for row in range(length):
        depth = depth_ref[row : row + 1]
        counts[row * bins : (row + 1) * bins, :width] = jnp.where(depth == value, 1.0, 0.0).astype(BF16)
        counts[row * bins : (row + 1) * bins, width:] = jnp.where(depth > value, 1.0, 0.0).astype(BF16)
    before = lax.broadcasted_iota(jnp.int32, (width, width), 0)
    after = lax.broadcasted_iota(jnp.int32, (width, width), 1)
    table[:width] = jnp.where(before < after, 1.0, 0.0).astype(BF16)
    table[width:] = jnp.ones((width, width), BF16)
    ranks = nn(counts[...], table[...])
    for row in range(length):
        here = jnp.where(depth_ref[row : row + 1] == value, ranks[row * bins : (row + 1) * bins], 0.0)
        place = jnp.sum(here, axis=0, keepdims=True)
        place_ref[row : row + 1] = place if row % 2 == 0 else (width - 1.0) - place

    for copy in copies[:-1]:
        copy.wait()
    level = stacks + lax.broadcasted_iota(jnp.int32, (thin, width), 0).astype(F32)

    def body(i, _):
        sorted_rows = []
        for k in range(2):
            row = 2 * i + k
            wet = level < depth_ref[pl.ds(row, 1)]
            cells = [
                jnp.where(wet, halves_of(held, kind * thin * length + row, thin, length), 0.0).astype(BF16)
                for kind in range(kinds)
            ]
            sorted_rows.append(nt(jnp.concatenate(cells, axis=0), one_hot(place_ref[pl.ds(row, 1)])))
        for k in range(2):
            for kind in range(kinds):
                at = kind * thin
                deep = sorted_rows[1 - k][at + stacks : at + 2 * stacks]
                value = sorted_rows[k][at : at + stacks] + pltpu.roll(deep, stacks // 2, 0)
                put_halves(packed, kind * stacks * length + 2 * i + k, stacks, length, value)
        return 0

    lax.fori_loop(0, length // 2, body, 0, unroll=8)
    copies[-1].wait()
    for half in range(halves):
        inside = slice(half * rows, (half + 1) * rows)
        for kind in range(kinds):
            block = plain[kind].reshape(stacks, length, width)
            sent_ref[half, :, kind, 0] = block[:, inside].astype(BF16)
            for part in range(packed.shape[0]):
                at = kind * stacks * length
                block = packed[part, at : at + stacks * length].reshape(stacks, length, 128)
                sent_ref[half, :, kind, 1, :, part * 128 : (part + 1) * 128] = block[:, inside].astype(BF16)


def finish_kernel(
    x_ref, arrived_ref, place_ref, land_ref, bottom_ref, result_ref, held, spread, field, arrivals, leaving
):
    kinds, levels, length, width = x_ref.shape
    copies = [pltpu.make_async_copy(x_ref.at[kind], field.at[kind], arrivals.at[kind]) for kind in range(kinds)]
    for copy in copies:
        copy.start()
    halves, stacks, _, _, rows, _ = arrived_ref.shape
    thin = levels - stacks
    each = stacks * kinds * rows
    for half in range(halves):
        for part in range(held.shape[0]):
            block = arrived_ref[half, :, :, 1, :, part * 128 : (part + 1) * 128]
            held[part, half * each : (half + 1) * each] = block.astype(F32).reshape(each, 128)

    def body(i, _):
        half = i // (rows // 2)
        row = 2 * i - half * rows
        cells = []
        for k in range(2):
            for kind in range(kinds):
                cells.append(halves_of(held, half * each + kind * rows + row + k, stacks, kinds * rows))
        cells = jnp.concatenate(cells, axis=0).astype(BF16)
        for k in range(2):
            value = nn(cells, one_hot(place_ref[pl.ds(2 * i + k, 1)]))
            for kind in range(kinds):
                near = (k * kinds + kind) * stacks
                other = ((1 - k) * kinds + kind) * stacks
                at = kind * thin * length + 2 * i + k
                put_halves(spread, at, stacks, length, value[near : near + stacks])
                deep = pltpu.roll(value[other : other + stacks], stacks // 2, 0)
                put_halves(spread, at + stacks * length, stacks, length, deep)
        return 0

    lax.fori_loop(0, length // 2, body, 0, unroll=8)
    depth = jnp.where(land_ref[...] == 1, bottom_ref[...], 0)
    sent = []
    for kind in range(kinds):
        copies[kind].wait()
        for level in range(levels):
            if level < stacks:
                change = jnp.concatenate(
                    [arrived_ref[half, level, kind, 0] for half in range(halves)], axis=0
                ).astype(F32)
            else:
                at = (kind * thin + level - stacks) * length
                change = jnp.concatenate(
                    [spread[part, at : at + length] for part in range(spread.shape[0])], axis=1
                )
            field[kind, level] = jnp.where(level < depth, field[kind, level] + change, 0.0)
            if level % stacks == stacks - 1:
                block = pl.ds(level + 1 - stacks, stacks)
                sent.append(
                    pltpu.make_async_copy(
                        field.at[kind, block], result_ref.at[kind, block], leaving.at[len(sent)]
                    )
                )
                sent[-1].start()
    for copy in sent:
        copy.wait()


def source_kernel(
    rows,
    cells_ref,
    table_ref,
    factors_hbm,
    in_ref,
    mid_hbm,
    bias_ref,
    out_ref,
    middle_ref,
    spread_ref,
    held,
    factors_ref,
    mid_ref,
    arrivals,
):
    _, kinds, width = cells_ref.shape
    ahead = rows + 2
    weights = (in_ref, mid_ref, bias_ref, out_ref)
    copies = [
        pltpu.make_async_copy(mid_hbm, mid_ref, arrivals.at[0]),
        pltpu.make_async_copy(factors_hbm, factors_ref, arrivals.at[1]),
    ]
    for copy in copies:
        copy.start()

    def cell(level, row):
        if level == 0:
            return cells_ref[row]
        return spread_ref[(level - 1) * rows + row]

    def spread_out(i):
        row = 2 * i
        cells = jnp.concatenate([cells_ref[rows + row], cells_ref[rows + row + 1]], axis=0)
        for k in range(2):
            value = nn(cells, table_ref[row + 2 + k]).astype(BF16)
            spread_ref[row + k] = value[k * kinds : (k + 1) * kinds]
            spread_ref[rows + row + k] = value[(1 - k) * kinds : (2 - k) * kinds]

    def sources(i):
        row = 2 * i
        cells = [cells_ref[row], cells_ref[row + 1], cells_ref[rows + row], cells_ref[rows + row + 1]]
        result = network(jnp.concatenate(cells, axis=1), *[ref[...] for ref in weights])
        held[i] = result.astype(BF16)

    def move(i):
        row = 2 * i
        result = held[i]
        packed = jnp.concatenate(
            [result[:, 2 * width : 3 * width], result[:, 3 * width :]], axis=0
        )
        for k in range(2):
            value = nn(packed, table_ref[row + 2 + k])
            pieces = [
                result[:, k * width : (k + 1) * width].astype(F32),
                value[k * kinds : (k + 1) * kinds],
                value[(1 - k) * kinds : (2 - k) * kinds],
            ]
            for level in range(3):
                factors = factors_ref[level * ahead + row + 1 + k]
                above, below = factors[1:2], factors[2:3]
                if k == 0:
                    above = jnp.where(row > 0, above, 0.0)
                else:
                    below = jnp.where(row + 2 < rows, below, 0.0)
                middle_ref[level * rows + row + k] = advance(
                    cell(level, row + k).astype(F32),
                    cell(level, jnp.maximum(row + k - 1, 0)).astype(F32),
                    cell(level, jnp.minimum(row + k + 1, rows - 1)).astype(F32),
                    pieces[level],
                    factors,
                    above,
                    below,
                )

    def body(i, _):
        move(i - 1)
        sources(i)
        return 0

    for i in range(rows // 2):
        spread_out(i)
    copies[0].wait()
    sources(0)
    copies[1].wait()
    lax.fori_loop(1, rows // 2, body, 0)
    move(rows // 2 - 1)


def step_kernel(
    rows,
    cells_ref,
    spread_ref,
    partial_ref,
    top_ref,
    bottom_ref,
    table_ref,
    factors_ref,
    in_ref,
    mid_ref,
    bias_ref,
    out_ref,
    change_ref,
    middle,
    packed,
    held,
    scratch,
):
    _, kinds, width = cells_ref.shape
    ahead = rows + 2
    weights = (in_ref, mid_ref, bias_ref, out_ref)

    def run(cells):
        return network(jnp.concatenate(cells, axis=1), *[ref[...] for ref in weights]).astype(BF16)

    for level in range(3):
        for row in range(1, rows - 1):
            middle[level * ahead + 1 + row] = partial_ref[level * rows + row]


    def put_together(row, thin):
        values = [nt(thin[k], table_ref[row + 2 + k]) for k in range(2)]
        return [values[k][:kinds] + values[1 - k][kinds:] for k in range(2)]

    def pack(i):
        row = 2 * i
        thin = [
            jnp.concatenate(
                [middle[level * ahead + 1 + row + k].astype(BF16) for level in (1, 2)], axis=0
            )
            for k in range(2)
        ]
        values = put_together(row, thin)
        for k in range(2):
            packed[row + k] = values[k].astype(BF16)

    def sources_of(i):
        row = 2 * i
        cells = [middle[1 + row + k].astype(BF16) for k in range(2)]
        held[i] = run(cells + [packed[row], packed[row + 1]])

    def move(i):
        row = 2 * i
        result = held[i]
        thin_sources = jnp.concatenate(
            [result[:, 2 * width : 3 * width], result[:, 3 * width :]], axis=0
        )
        changes = []
        for k in range(2):
            value = nn(thin_sources, table_ref[row + 2 + k])
            pieces = [
                result[:, k * width : (k + 1) * width].astype(F32),
                value[k * kinds : (k + 1) * kinds],
                value[(1 - k) * kinds : (2 - k) * kinds],
            ]
            for level in range(3):
                at = level * ahead + 1 + row + k
                factors = factors_ref[at]
                value = advance(
                    middle[at],
                    middle[at - 1],
                    middle[at + 1],
                    pieces[level],
                    factors,
                    factors[1:2],
                    factors[2:3],
                )
                if level == 0:
                    first = cells_ref[row + k]
                else:
                    first = spread_ref[(level - 1) * rows + row + k]
                changes.append(value - factors[6:7] * first.astype(F32))
        thin = [
            jnp.concatenate([changes[3 * k + 1].astype(BF16), changes[3 * k + 2].astype(BF16)], axis=0)
            for k in range(2)
        ]
        values = put_together(row, thin)
        for k in range(2):
            put_halves(scratch, row + k, kinds, rows, changes[3 * k])
            put_halves(scratch, rows * kinds + row + k, kinds, rows, values[k])

    def turn(i):
        return (i + 1) % (rows // 2)

    def body(i, _):
        move(turn(i - 1))
        sources_of(turn(i))
        return 0

    for i in range(1, rows // 2 - 1):
        pack(i)
    edges = [
        [top_ref[1], top_ref[2], top_ref[3]],
        [bottom_ref[0], bottom_ref[2], bottom_ref[3]],
    ]
    result = run(edges[0] + edges[1])
    for k in range(2):
        packed_cells = jnp.concatenate(edges[k][1:], axis=0)
        at = 3 * k * width
        packed_sources = jnp.concatenate(
            [result[:, at + width : at + 2 * width], result[:, at + 2 * width : at + 3 * width]], axis=0
        )
        near = nn(jnp.concatenate([packed_cells, packed_sources], axis=0), table_ref[[1, rows + 2][k]])
        far = nn(packed_cells, table_ref[[0, rows + 3][k]])
        near_at = [[1, 0], [0, 1]][k]
        far_at = [[0, 1], [1, 0]][k]
        for level in range(3):
            inside = level * rows + k * (rows - 1)
            if level == 0:
                own = edges[k][0].astype(F32)
                other = (top_ref[0] if k == 0 else bottom_ref[1]).astype(F32)
                sources = result[:, at : at + width].astype(F32)
                inner = cells_ref[k * (rows - 1)].astype(F32)
            else:
                place = near_at[level - 1] * kinds
                own = near[place : place + kinds]
                sources = near[2 * kinds + place : 3 * kinds + place]
                place = far_at[level - 1] * kinds
                other = far[place : place + kinds]
                inner = spread_ref[(level - 1) * rows + k * (rows - 1)].astype(F32)
            row = level * ahead + k * (ahead - 1)
            factors = factors_ref[row]
            middle[row] = advance(
                own,
                other if k == 0 else inner,
                inner if k == 0 else other,
                sources,
                factors,
                factors[1:2],
                factors[2:3],
            )
            row = level * ahead + 1 + k * (rows - 1)
            middle[row] = partial_ref[inside] + factors_ref[row][1 + k : 2 + k] * own
    sources_of(1)
    pack(0)
    pack(rows // 2 - 1)
    lax.fori_loop(1, rows // 2, body, 0)
    move(0)
    for level in range(2):
        for part in range(scratch.shape[0]):
            block = scratch[part, level * rows * kinds : (level + 1) * rows * kinds, :]
            change_ref[:, level, :, part * 128 : (part + 1) * 128] = block.reshape(kinds, rows, 128).astype(BF16)


HBM = pltpu.HBM


def kernel_call(kernel, outs, scratch, flops, name, places=None, result_places=None):
    def specs(given):
        return [pl.BlockSpec(memory_space=place or pltpu.VMEM) for place in given]

    spaces = {} if places is None else {"in_specs": specs(places)}
    if result_places is not None:
        spaces["out_specs"] = specs(result_places)[0]
    return pl.pallas_call(
        kernel,
        out_shape=outs,
        **spaces,
        scratch_shapes=scratch,
        cost_estimate=pl.CostEstimate(flops=flops, bytes_accessed=4_000_000, transcendentals=0),
        compiler_params=pltpu.CompilerParams(vmem_limit_bytes=24 * 2**20),
        name=name,
    )


def factors_of(east, north, depth, level):
    wet = (level[:, None, None] < depth[None]).astype(F32)
    opened = time_step * wet[:, :-1] * wet[:, 1:]
    plus = opened * (jnp.maximum(east[:, :-1], 0.0) + diffusion)
    minus = opened * (jnp.minimum(east[:, :-1], 0.0) - diffusion)
    inner = wet[:, 1:-1]
    flow = jnp.pad(north[:, 1:-1], ((0, 0), (0, 0), (1, 0)))
    sides = jnp.pad(inner, ((0, 0), (0, 0), (1, 1)))
    opened = time_step * sides[..., :-1] * sides[..., 1:]
    right = opened * (jnp.maximum(flow, 0.0) + diffusion)
    left = opened * (jnp.minimum(flow, 0.0) - diffusion)
    own = inner + (minus[:, :-1] - plus[:, 1:]) + (left[..., :-1] - right[..., 1:])
    return jnp.stack(
        [
            own,
            plus[:, :-1],
            -minus[:, 1:],
            right[..., :-1],
            -left[..., 1:],
            time_step * inner,
            inner,
            jnp.zeros_like(inner),
        ],
        axis=2,
    )


def with_halo(value, sides, width):
    for axis, dim in sides:
        size, length = (lax.axis_size(axis), value.shape[dim])
        up = [(i, (i + 1) % size) for i in range(size - 1)]
        down = [(j, i) for i, j in up]
        last = lax.slice_in_dim(value, length - width, length, axis=dim)
        initial = lax.slice_in_dim(value, 0, width, axis=dim)
        before = lax.ppermute(last, axis, up)
        after = lax.ppermute(initial, axis, down)
        value = jnp.concatenate([before, value, after], axis=dim)
    return value


def as_sent(value):
    return jax.tree.map(lambda a: a.astype(jnp.bfloat16) if a.dtype == jnp.float32 else a, value)


def face_flux(behind_cells, ahead_cells, flow_speed, opened):
    moved = jnp.maximum(flow_speed, 0.0) * behind_cells + jnp.minimum(flow_speed, 0.0) * ahead_cells
    return opened * (moved - diffusion * (ahead_cells - behind_cells))


def plain_network(inputs, in_weight, in_bias, mid_weight, mid_bias, out_weight):
    kinds, depth, rows, cols = inputs.shape
    cells = depth * rows * cols
    turns = math.gcd(cells, 8)
    blocked = jnp.moveaxis(inputs.reshape(kinds, turns, cells // turns), 1, 0)

    def one_block(cell_block):
        first_hidden = (
            jnp.einsum("tn,th->nh", cell_block, in_weight, preferred_element_type=jnp.float32)
            + in_bias
        )
        first_hidden = jax.nn.silu(first_hidden).astype(jnp.bfloat16)
        second_hidden = (
            jnp.einsum("nh,hk->nk", first_hidden, mid_weight, preferred_element_type=jnp.float32)
            + mid_bias
        )
        second_hidden = jax.nn.silu(second_hidden).astype(jnp.bfloat16)
        return jnp.einsum(
            "nh,ht->tn", second_hidden, out_weight, preferred_element_type=jnp.float32
        ).astype(jnp.bfloat16)

    result = jnp.moveaxis(lax.map(one_block, blocked), 0, 1)
    return result.reshape(result.shape[0], depth, rows, cols)


def plain_body(
    tracers,
    east_speed,
    north_speed,
    land_mask,
    bottom_level,
    in_weight,
    in_bias,
    mid_weight,
    mid_bias,
    out_weight,
):
    levels = east_speed.shape[0]
    depth = jnp.arange(levels, dtype=jnp.int32)[:, None, None]
    wet_cells = ((land_mask[None] == 1) & (depth < bottom_level[None])).astype(jnp.float32)
    geometry = with_halo(
        jnp.stack([east_speed, wet_cells]).astype(jnp.bfloat16), (("tile", 2),), 1
    ).astype(jnp.float32)
    flow_x = geometry[0, :, :-1]
    wet_x = geometry[1]
    opened_x = wet_x[:, :-1] * wet_x[:, 1:]
    flow_y = jnp.pad(north_speed, ((0, 0), (0, 0), (1, 0)))
    wet_y = jnp.pad(wet_cells, ((0, 0), (0, 0), (1, 1)))
    opened_y = wet_y[..., :-1] * wet_y[..., 1:]
    field = tracers
    for step in range(STEPS):
        padded = with_halo(as_sent(field), (("tile", 2),), 1).astype(field.dtype)
        inputs = field.astype(jnp.bfloat16)
        local_sources = plain_network(
            lax.all_to_all(inputs, "tracer", split_axis=2, concat_axis=0, tiled=True),
            in_weight,
            in_bias,
            mid_weight,
            mid_bias,
            out_weight,
        )
        sources = lax.all_to_all(local_sources, "tracer", split_axis=0, concat_axis=2, tiled=True)
        x_flux = face_flux(padded[:, :, :-1], padded[:, :, 1:], flow_x, opened_x)
        cells_y = jnp.pad(field, ((0, 0), (0, 0), (0, 0), (1, 1)))
        y_flux = face_flux(cells_y[..., :-1], cells_y[..., 1:], flow_y, opened_y)
        tendency = x_flux[:, :, :-1] - x_flux[:, :, 1:] + (y_flux[..., :-1] - y_flux[..., 1:])
        field = wet_cells[None] * (field + time_step * (tendency + sources.astype(jnp.float32)))
    return field


def split_parts(value, count):
    parts = []
    for _ in range(count):
        parts.append(value.astype(BF16))
        value = value - parts[-1].astype(F32)
    return parts


def body(
    tracers,
    east_speed,
    north_speed,
    land_mask,
    bottom_level,
    in_weight,
    in_bias,
    mid_weight,
    mid_bias,
    out_weight,
):
    arguments = (
        tracers,
        east_speed,
        north_speed,
        land_mask,
        bottom_level,
        in_weight,
        in_bias,
        mid_weight,
        mid_bias,
        out_weight,
    )
    kinds, levels, length, columns = tracers.shape
    tiles, group = lax.axis_size("tile"), lax.axis_size("tracer")
    halves = 2
    stacks = group // halves
    rows = length // halves
    own = lax.axis_index("tracer")
    half, stack = own // stacks, own % stacks
    all_kinds = kinds * group
    thin = levels - stacks
    parts = columns // 128

    sent, place = kernel_call(
        pack_kernel,
        [
            jax.ShapeDtypeStruct((halves, stacks, kinds, 2, rows, columns), BF16),
            jax.ShapeDtypeStruct((length, columns), F32),
        ],
        [
            pltpu.VMEM((length, columns), F32),
            pltpu.VMEM((length * 32, 2 * columns), BF16),
            pltpu.VMEM((2 * columns, columns), BF16),
            pltpu.VMEM((parts, kinds * thin * length, 128), F32),
            pltpu.VMEM((kinds, stacks * length, columns), F32),
            pltpu.VMEM((parts, kinds * stacks * length, 128), F32),
            pltpu.SemaphoreType.DMA((kinds * parts + 1,)),
        ],
        2 * length * columns * columns * (32 + 64),
        "pack",
        [HBM, None, None],
    )(tracers.reshape(kinds, levels * length, columns), land_mask, bottom_level)
    sent = sent.reshape(group, kinds, 2, rows, columns)
    cells = lax.all_to_all(sent, "tracer", split_axis=0, concat_axis=0, tiled=True)
    cells = cells.reshape(all_kinds, 2, rows, columns)

    east_speed, north_speed, land_mask, sent = lax.optimization_barrier(
        (east_speed, north_speed, land_mask, sent)
    )
    depth = jnp.where(land_mask == 1, bottom_level, 0).astype(F32)
    level_list = [stack, stacks + stack, 2 * stacks + (stack + stacks // 2) % stacks]

    side, position = stack // (stacks // 2), stack % (stacks // 2)

    def own_levels(value):
        value = value.reshape(2 * levels // stacks, stacks // 2, length, columns)
        value = lax.dynamic_slice_in_dim(value, position, 1, 1)[:, 0]
        return jnp.where(
            side == 0,
            jnp.stack([value[0], value[2], value[5]]),
            jnp.stack([value[1], value[3], value[4]]),
        )

    geometry = [own_levels(east_speed), own_levels(north_speed), depth[None], place[None]]

    def at(tile, part, position):
        return tile * group + part * stacks + position

    across, within = [], []
    for position in range(stacks):
        for tile in range(tiles):
            within.append((at(tile, 0, position), at(tile, 1, position)))
            if tile + 1 < tiles:
                across.append((at(tile, 1, position), at(tile + 1, 0, position)))
    back = [(j, i) for i, j in across]
    axes = ("tile", "tracer")
    edge = jnp.concatenate(
        [lax.dynamic_slice_in_dim(value, half * (length - 2), 2, 1) for value in geometry], axis=0
    )
    arrived = lax.ppermute(edge, axes, across + back)
    arrived = [arrived[:3], arrived[3:6], arrived[6:7], arrived[7:8]]

    def widened(value, outside):
        return jnp.where(
            half == 0,
            jnp.concatenate([outside, value[:, : rows + 2]], axis=1),
            jnp.concatenate([value[:, rows - 2 :], outside], axis=1),
        )

    east, north, wide_depth, wide_place = [widened(*pair) for pair in zip(geometry, arrived)]
    factors = factors_of(east, north, wide_depth[0], jnp.stack(level_list).astype(F32)).reshape(
        3 * (rows + 2), 8, columns
    )
    slots = jnp.arange(columns, dtype=jnp.int32).astype(F32)
    table = (slots[None, :, None] == wide_place[0][:, None, :]).astype(BF16)

    in_parts = jnp.stack(split_parts(0.5 * in_bias, 3) + [jnp.zeros(in_bias.shape, BF16)] * 13, axis=1)
    weights = (
        jnp.concatenate([(0.5 * in_weight.astype(F32)).astype(BF16).T, in_parts], axis=1),
        (0.5 * mid_weight.astype(F32)).astype(BF16).T,
        jnp.broadcast_to(0.5 * mid_bias[:, None], mid_bias.shape + (128,)),
        out_weight.T,
    )

    hidden = in_weight.shape[1]
    pieces = 2 * rows
    per_piece = 2 * columns * hidden * (hidden + 2 * all_kinds)
    turned, first, last = kernel_call(
        functools.partial(turn_kernel, rows),
        [
            jax.ShapeDtypeStruct((pieces, all_kinds, columns), BF16),
            jax.ShapeDtypeStruct((4, all_kinds, columns), BF16),
            jax.ShapeDtypeStruct((4, all_kinds, columns), BF16),
        ],
        [pltpu.VMEM((parts, all_kinds * rows, 128), F32)],
        1_000_000,
        "turn",
    )(cells)
    top = lax.ppermute(last, axes, within + across)
    bottom = lax.ppermute(first, axes, [(j, i) for i, j in within] + back)
    partial, spread = kernel_call(
        functools.partial(source_kernel, rows),
        [
            jax.ShapeDtypeStruct((3 * rows, all_kinds, columns), F32),
            jax.ShapeDtypeStruct((2 * rows, all_kinds, columns), BF16),
        ],
        [
            pltpu.VMEM((rows // 2, all_kinds, 4 * columns), BF16),
            pltpu.VMEM(factors.shape, F32),
            pltpu.VMEM(mid_weight.shape, BF16),
            pltpu.SemaphoreType.DMA((2,)),
        ],
        pieces * per_piece,
        "sources",
        [None, None, HBM, None, HBM, None, None],
    )(turned, table, factors, *weights)
    change = kernel_call(
        functools.partial(step_kernel, rows),
        jax.ShapeDtypeStruct(cells.shape, BF16),
        [
            pltpu.VMEM((3 * (rows + 2), all_kinds, columns), F32),
            pltpu.VMEM((rows, all_kinds, columns), BF16),
            pltpu.VMEM((rows // 2, all_kinds, 4 * columns), BF16),
            pltpu.VMEM((parts, 2 * rows * all_kinds, 128), F32),
        ],
        pieces * per_piece,
        "steps",
    )(turned, spread, partial, top, bottom, table, factors, *weights)

    depth, change = lax.optimization_barrier((depth, change))
    level = jnp.arange(levels, dtype=jnp.int32).astype(F32)
    count = jnp.sum((level[:, None, None] < depth[None]).astype(F32), axis=2)
    deep = jnp.roll(count[2 * stacks :], -(stacks // 2), axis=0)
    deep = jnp.flip(deep.reshape(stacks, length // 2, 2), axis=2).reshape(stacks, length)
    fullest = jnp.full((8, 128), jnp.max(count[stacks : 2 * stacks] + deep))
    for step in (1, tiles // 4):
        others = []
        for times in (1, 2, 3):
            pairs = [(tile, tile ^ (step * times)) for tile in range(tiles)]
            others.append(lax.ppermute(fullest, "tile", pairs))
        fullest = functools.reduce(jnp.maximum, others, fullest)
    excess = fullest[0, 0] > columns

    change = change.reshape(group, kinds, 2, rows, columns)
    change = lax.all_to_all(change, "tracer", split_axis=0, concat_axis=0, tiled=True)
    change = change.reshape(halves, stacks, kinds, 2, rows, columns)

    def finish(change, place, arguments):
        return kernel_call(
            finish_kernel,
            jax.ShapeDtypeStruct(tracers.shape, F32),
            [
                pltpu.VMEM((parts, group * kinds * rows, 128), F32),
                pltpu.VMEM((parts, kinds * thin * length, 128), F32),
                pltpu.VMEM(tracers.shape, F32),
                pltpu.SemaphoreType.DMA((kinds,)),
                pltpu.SemaphoreType.DMA((kinds * levels // stacks,)),
            ],
            2 * length * columns * columns * 32,
            "finish",
            [HBM, None, None, None, None],
            [HBM],
        )(arguments[0], change, place, arguments[3], arguments[4])

    def in_full(change, place, arguments):
        return plain_body(*arguments)

    return lax.cond(excess, in_full, finish, change, place, arguments)


def solution(mesh):
    return jax.shard_map(
        body,
        mesh=mesh,
        in_specs=(
            P("tracer", None, "tile", None),
            P(None, "tile", None),
            P(None, "tile", None),
            P("tile", None),
            P("tile", None),
            P(),
            P(),
            P(),
            P(),
            P(),
        ),
        out_specs=P("tracer", None, "tile", None),
        check_vma=False,
    )
```

```python
import functools
import math

import jax
import jax.numpy as jnp
from jax import lax
from jax.experimental import pallas as pl
from jax.experimental.pallas import tpu as pltpu
from jax.sharding import PartitionSpec as P

STEPS = 2
diffusion = 0.2
time_step = 0.2
GROUP = 4

BF16 = jnp.bfloat16
F32 = jnp.float32


def silu_of_half(half):
    return (half + half * jnp.tanh(half)).astype(BF16)


def network(cells, in_weight, mid_weight, mid_bias, out_weight):
    lanes = cells.shape[1]
    cells = jnp.concatenate([cells, jnp.ones((16, lanes), BF16)], axis=0)
    hidden = silu_of_half(jnp.dot(in_weight, cells, preferred_element_type=F32))
    hidden = jnp.dot(mid_weight, hidden, preferred_element_type=F32)
    hidden = silu_of_half(hidden + jnp.concatenate([mid_bias] * (lanes // 128), axis=1))
    return jnp.dot(out_weight, hidden, preferred_element_type=F32)


def turn_kernel(rows, x_ref, turned_ref, first_ref, last_ref, scratch):
    kinds, levels = x_ref.shape[:2]
    for level in range(levels):
        for part in range(scratch.shape[0]):
            block = x_ref[:, level, :, part * 128 : (part + 1) * 128]
            scratch[part] = block.astype(F32).reshape(kinds * rows, 128)
        for row in range(rows):
            picked = [scratch[part, pl.ds(row, kinds, stride=rows), :] for part in range(scratch.shape[0])]
            piece = jnp.concatenate(picked, axis=1).astype(BF16)
            turned_ref[level * rows + row] = piece
            if row < 2:
                first_ref[level * 2 + row] = piece
            if row >= rows - 2:
                last_ref[level * 2 + row - rows + 2] = piece


def advance(here, above, below, sources, factors, from_above, from_below):
    width = here.shape[1]
    west = pltpu.roll(here, 1, 1)
    east = pltpu.roll(here, width - 1, 1)
    result = factors[0:1] * here + from_above * above + from_below * below
    return result + factors[3:4] * west + factors[4:5] * east + factors[5:6] * sources


def nt(rows, table):
    return lax.dot_general(rows, table, (((1,), (1,)), ((), ())), preferred_element_type=F32)


def nn(rows, table):
    return jnp.dot(rows, table, preferred_element_type=F32)


def one_hot(place):
    width = place.shape[1]
    slots = lax.broadcasted_iota(jnp.int32, (width, width), 0).astype(F32)
    return jnp.where(slots == place, 1.0, 0.0).astype(BF16)


def halves_of(ref, start, size, stride):
    return jnp.concatenate(
        [ref[part, pl.ds(start, size, stride=stride), :] for part in range(ref.shape[0])], axis=1
    )


def put_halves(ref, start, size, stride, value):
    for part in range(ref.shape[0]):
        ref[part, pl.ds(start, size, stride=stride), :] = value[:, part * 128 : (part + 1) * 128]


def pack_kernel(
    x_ref, land_ref, bottom_ref, sent_ref, place_ref, depth_ref, counts, table, held, plain, packed, arrivals
):
    kinds, _, width = x_ref.shape
    length = land_ref.shape[0]
    halves, stacks, _, _, rows, _ = sent_ref.shape
    levels = x_ref.shape[1] // length
    thin = levels - stacks
    parts = held.shape[0]
    copies = []
    for kind in range(kinds):
        for part in range(parts):
            copies.append(
                pltpu.make_async_copy(
                    x_ref.at[kind, pl.ds(stacks * length, thin * length), pl.ds(part * 128, 128)],
                    held.at[part, pl.ds(kind * thin * length, thin * length)],
                    arrivals.at[len(copies)],
                )
            )
    copies.append(
        pltpu.make_async_copy(x_ref.at[:, pl.ds(0, stacks * length)], plain, arrivals.at[len(copies)])
    )
    for copy in copies:
        copy.start()
    depth_ref[...] = jnp.where(land_ref[...] == 1, bottom_ref[...], 0).astype(F32)
    bins = 32
    value = lax.broadcasted_iota(jnp.int32, (bins, width), 0).astype(F32)
    for row in range(length):
        depth = depth_ref[row : row + 1]
        counts[row * bins : (row + 1) * bins, :width] = jnp.where(depth == value, 1.0, 0.0).astype(BF16)
        counts[row * bins : (row + 1) * bins, width:] = jnp.where(depth > value, 1.0, 0.0).astype(BF16)
    before = lax.broadcasted_iota(jnp.int32, (width, width), 0)
    after = lax.broadcasted_iota(jnp.int32, (width, width), 1)
    table[:width] = jnp.where(before < after, 1.0, 0.0).astype(BF16)
    table[width:] = jnp.ones((width, width), BF16)
    ranks = nn(counts[...], table[...])
    for row in range(length):
        here = jnp.where(depth_ref[row : row + 1] == value, ranks[row * bins : (row + 1) * bins], 0.0)
        place = jnp.sum(here, axis=0, keepdims=True)
        place_ref[row : row + 1] = place if row % 2 == 0 else (width - 1.0) - place

    for copy in copies[:-1]:
        copy.wait()
    level = stacks + lax.broadcasted_iota(jnp.int32, (thin, width), 0).astype(F32)

    def body(i, _):
        sorted_rows = []
        for k in range(2):
            row = 2 * i + k
            wet = level < depth_ref[pl.ds(row, 1)]
            cells = [
                jnp.where(wet, halves_of(held, kind * thin * length + row, thin, length), 0.0).astype(BF16)
                for kind in range(kinds)
            ]
            sorted_rows.append(nt(jnp.concatenate(cells, axis=0), one_hot(place_ref[pl.ds(row, 1)])))
        for k in range(2):
            for kind in range(kinds):
                at = kind * thin
                deep = sorted_rows[1 - k][at + stacks : at + 2 * stacks]
                value = sorted_rows[k][at : at + stacks] + pltpu.roll(deep, stacks // 2, 0)
                put_halves(packed, kind * stacks * length + 2 * i + k, stacks, length, value)
        return 0

    lax.fori_loop(0, length // 2, body, 0, unroll=8)
    copies[-1].wait()
    for half in range(halves):
        inside = slice(half * rows, (half + 1) * rows)
        for kind in range(kinds):
            block = plain[kind].reshape(stacks, length, width)
            sent_ref[half, :, kind, 0] = block[:, inside].astype(BF16)
            for part in range(packed.shape[0]):
                at = kind * stacks * length
                block = packed[part, at : at + stacks * length].reshape(stacks, length, 128)
                sent_ref[half, :, kind, 1, :, part * 128 : (part + 1) * 128] = block[:, inside].astype(BF16)


def finish_kernel(
    x_ref, arrived_ref, place_ref, land_ref, bottom_ref, result_ref, held, spread, field, arrivals, leaving
):
    kinds, levels, length, width = x_ref.shape
    copies = [pltpu.make_async_copy(x_ref.at[kind], field.at[kind], arrivals.at[kind]) for kind in range(kinds)]
    for copy in copies:
        copy.start()
    halves, stacks, _, _, rows, _ = arrived_ref.shape
    thin = levels - stacks
    each = stacks * kinds * rows
    for half in range(halves):
        for part in range(held.shape[0]):
            block = arrived_ref[half, :, :, 1, :, part * 128 : (part + 1) * 128]
            held[part, half * each : (half + 1) * each] = block.astype(F32).reshape(each, 128)

    def body(i, _):
        half = i // (rows // 2)
        row = 2 * i - half * rows
        cells = []
        for k in range(2):
            for kind in range(kinds):
                cells.append(halves_of(held, half * each + kind * rows + row + k, stacks, kinds * rows))
        cells = jnp.concatenate(cells, axis=0).astype(BF16)
        for k in range(2):
            value = nn(cells, one_hot(place_ref[pl.ds(2 * i + k, 1)]))
            for kind in range(kinds):
                near = (k * kinds + kind) * stacks
                other = ((1 - k) * kinds + kind) * stacks
                at = kind * thin * length + 2 * i + k
                put_halves(spread, at, stacks, length, value[near : near + stacks])
                deep = pltpu.roll(value[other : other + stacks], stacks // 2, 0)
                put_halves(spread, at + stacks * length, stacks, length, deep)
        return 0

    lax.fori_loop(0, length // 2, body, 0, unroll=8)
    depth = jnp.where(land_ref[...] == 1, bottom_ref[...], 0)
    sent = []
    for kind in range(kinds):
        copies[kind].wait()
        for level in range(levels):
            if level < stacks:
                change = jnp.concatenate(
                    [arrived_ref[half, level, kind, 0] for half in range(halves)], axis=0
                ).astype(F32)
            else:
                at = (kind * thin + level - stacks) * length
                change = jnp.concatenate(
                    [spread[part, at : at + length] for part in range(spread.shape[0])], axis=1
                )
            field[kind, level] = jnp.where(level < depth, field[kind, level] + change, 0.0)
            if level % stacks == stacks - 1:
                block = pl.ds(level + 1 - stacks, stacks)
                sent.append(
                    pltpu.make_async_copy(
                        field.at[kind, block], result_ref.at[kind, block], leaving.at[len(sent)]
                    )
                )
                sent[-1].start()
    for copy in sent:
        copy.wait()


def source_kernel(
    rows,
    cells_ref,
    place_ref,
    factors_ref,
    in_ref,
    mid_ref,
    bias_ref,
    out_ref,
    middle_ref,
    spread_ref,
    table_ref,
    held,
):
    _, kinds, width = cells_ref.shape
    ahead = rows + 2
    weights = (in_ref, mid_ref, bias_ref, out_ref)

    def cell(level, row):
        if level == 0:
            return cells_ref[row]
        return spread_ref[(level - 1) * rows + row]

    def spread_out(i):
        row = 2 * i
        cells = jnp.concatenate([cells_ref[rows + row], cells_ref[rows + row + 1]], axis=0)
        for k in range(2):
            table = one_hot(place_ref[row + 2 + k : row + 3 + k])
            table_ref[row + 2 + k] = table
            value = nn(cells, table).astype(BF16)
            spread_ref[row + k] = value[k * kinds : (k + 1) * kinds]
            spread_ref[rows + row + k] = value[(1 - k) * kinds : (2 - k) * kinds]

    def sources(i):
        row = 2 * i
        cells = [cells_ref[row], cells_ref[row + 1], cells_ref[rows + row], cells_ref[rows + row + 1]]
        result = network(jnp.concatenate(cells, axis=1), *[ref[...] for ref in weights])
        held[i] = result.astype(BF16)

    def move(i):
        row = 2 * i
        result = held[i]
        packed = jnp.concatenate(
            [result[:, 2 * width : 3 * width], result[:, 3 * width :]], axis=0
        )
        for k in range(2):
            value = nn(packed, table_ref[row + 2 + k])
            pieces = [
                result[:, k * width : (k + 1) * width].astype(F32),
                value[k * kinds : (k + 1) * kinds],
                value[(1 - k) * kinds : (2 - k) * kinds],
            ]
            for level in range(3):
                factors = factors_ref[level * ahead + row + 1 + k]
                above, below = factors[1:2], factors[2:3]
                if k == 0:
                    above = jnp.where(row > 0, above, 0.0)
                else:
                    below = jnp.where(row + 2 < rows, below, 0.0)
                middle_ref[level * rows + row + k] = advance(
                    cell(level, row + k).astype(F32),
                    cell(level, jnp.maximum(row + k - 1, 0)).astype(F32),
                    cell(level, jnp.minimum(row + k + 1, rows - 1)).astype(F32),
                    pieces[level],
                    factors,
                    above,
                    below,
                )

    def body(i, _):
        move(i - 1)
        sources(i)
        return 0

    for i in range(rows // 2):
        spread_out(i)
    for row in (0, 1, rows + 2, rows + 3):
        table_ref[row] = one_hot(place_ref[row : row + 1])
    sources(0)
    lax.fori_loop(1, rows // 2, body, 0)
    move(rows // 2 - 1)


def step_kernel(
    rows,
    cells_ref,
    spread_ref,
    partial_ref,
    top_ref,
    bottom_ref,
    table_ref,
    factors_ref,
    in_ref,
    mid_ref,
    bias_ref,
    out_ref,
    change_ref,
    middle,
    packed,
    held,
    scratch,
):
    _, kinds, width = cells_ref.shape
    ahead = rows + 2
    weights = (in_ref, mid_ref, bias_ref, out_ref)

    def run(cells):
        return network(jnp.concatenate(cells, axis=1), *[ref[...] for ref in weights]).astype(BF16)

    for level in range(3):
        for row in range(1, rows - 1):
            middle[level * ahead + 1 + row] = partial_ref[level * rows + row]


    def put_together(row, thin):
        values = [nt(thin[k], table_ref[row + 2 + k]) for k in range(2)]
        return [values[k][:kinds] + values[1 - k][kinds:] for k in range(2)]

    def pack(i):
        row = 2 * i
        thin = [
            jnp.concatenate(
                [middle[level * ahead + 1 + row + k].astype(BF16) for level in (1, 2)], axis=0
            )
            for k in range(2)
        ]
        values = put_together(row, thin)
        for k in range(2):
            packed[row + k] = values[k].astype(BF16)

    def sources_of(i):
        row = 2 * i
        cells = [middle[1 + row + k].astype(BF16) for k in range(2)]
        held[i] = run(cells + [packed[row], packed[row + 1]])

    def move(i):
        row = 2 * i
        result = held[i]
        thin_sources = jnp.concatenate(
            [result[:, 2 * width : 3 * width], result[:, 3 * width :]], axis=0
        )
        changes = []
        for k in range(2):
            value = nn(thin_sources, table_ref[row + 2 + k])
            pieces = [
                result[:, k * width : (k + 1) * width].astype(F32),
                value[k * kinds : (k + 1) * kinds],
                value[(1 - k) * kinds : (2 - k) * kinds],
            ]
            for level in range(3):
                at = level * ahead + 1 + row + k
                factors = factors_ref[at]
                value = advance(
                    middle[at],
                    middle[at - 1],
                    middle[at + 1],
                    pieces[level],
                    factors,
                    factors[1:2],
                    factors[2:3],
                )
                if level == 0:
                    first = cells_ref[row + k]
                else:
                    first = spread_ref[(level - 1) * rows + row + k]
                changes.append(value - factors[6:7] * first.astype(F32))
        thin = [
            jnp.concatenate([changes[3 * k + 1].astype(BF16), changes[3 * k + 2].astype(BF16)], axis=0)
            for k in range(2)
        ]
        values = put_together(row, thin)
        for k in range(2):
            put_halves(scratch, row + k, kinds, rows, changes[3 * k])
            put_halves(scratch, rows * kinds + row + k, kinds, rows, values[k])

    def turn(i):
        return (i + 1) % (rows // 2)

    def body(i, _):
        move(turn(i - 1))
        sources_of(turn(i))
        return 0

    for i in range(1, rows // 2 - 1):
        pack(i)
    edges = [
        [top_ref[1], top_ref[2], top_ref[3]],
        [bottom_ref[0], bottom_ref[2], bottom_ref[3]],
    ]
    result = run(edges[0] + edges[1])
    for k in range(2):
        packed_cells = jnp.concatenate(edges[k][1:], axis=0)
        at = 3 * k * width
        packed_sources = jnp.concatenate(
            [result[:, at + width : at + 2 * width], result[:, at + 2 * width : at + 3 * width]], axis=0
        )
        near = nn(jnp.concatenate([packed_cells, packed_sources], axis=0), table_ref[[1, rows + 2][k]])
        far = nn(packed_cells, table_ref[[0, rows + 3][k]])
        near_at = [[1, 0], [0, 1]][k]
        far_at = [[0, 1], [1, 0]][k]
        for level in range(3):
            inside = level * rows + k * (rows - 1)
            if level == 0:
                own = edges[k][0].astype(F32)
                other = (top_ref[0] if k == 0 else bottom_ref[1]).astype(F32)
                sources = result[:, at : at + width].astype(F32)
                inner = cells_ref[k * (rows - 1)].astype(F32)
            else:
                place = near_at[level - 1] * kinds
                own = near[place : place + kinds]
                sources = near[2 * kinds + place : 3 * kinds + place]
                place = far_at[level - 1] * kinds
                other = far[place : place + kinds]
                inner = spread_ref[(level - 1) * rows + k * (rows - 1)].astype(F32)
            row = level * ahead + k * (ahead - 1)
            factors = factors_ref[row]
            middle[row] = advance(
                own,
                other if k == 0 else inner,
                inner if k == 0 else other,
                sources,
                factors,
                factors[1:2],
                factors[2:3],
            )
            row = level * ahead + 1 + k * (rows - 1)
            middle[row] = partial_ref[inside] + factors_ref[row][1 + k : 2 + k] * own
    sources_of(1)
    pack(0)
    pack(rows // 2 - 1)
    lax.fori_loop(1, rows // 2, body, 0, unroll=True)
    move(0)
    for level in range(2):
        for part in range(scratch.shape[0]):
            block = scratch[part, level * rows * kinds : (level + 1) * rows * kinds, :]
            change_ref[:, level, :, part * 128 : (part + 1) * 128] = block.reshape(kinds, rows, 128).astype(BF16)


HBM = pltpu.HBM


def kernel_call(kernel, outs, scratch, flops, name, places=None, result_places=None, memory=32):
    def specs(given):
        return [pl.BlockSpec(memory_space=place or pltpu.VMEM) for place in given]

    spaces = {} if places is None else {"in_specs": specs(places)}
    if result_places is not None:
        spaces["out_specs"] = specs(result_places)[0]
    return pl.pallas_call(
        kernel,
        out_shape=outs,
        **spaces,
        scratch_shapes=scratch,
        cost_estimate=pl.CostEstimate(flops=flops, bytes_accessed=4_000_000, transcendentals=0),
        compiler_params=pltpu.CompilerParams(vmem_limit_bytes=memory * 2**20),
        name=name,
    )


def factors_of(east, north, depth, level):
    wet = (level[:, None, None] < depth[None]).astype(F32)
    opened = time_step * wet[:, :-1] * wet[:, 1:]
    plus = opened * (jnp.maximum(east[:, :-1], 0.0) + diffusion)
    minus = opened * (jnp.minimum(east[:, :-1], 0.0) - diffusion)
    inner = wet[:, 1:-1]
    flow = jnp.pad(north[:, 1:-1], ((0, 0), (0, 0), (1, 0)))
    sides = jnp.pad(inner, ((0, 0), (0, 0), (1, 1)))
    opened = time_step * sides[..., :-1] * sides[..., 1:]
    right = opened * (jnp.maximum(flow, 0.0) + diffusion)
    left = opened * (jnp.minimum(flow, 0.0) - diffusion)
    own = inner + (minus[:, :-1] - plus[:, 1:]) + (left[..., :-1] - right[..., 1:])
    return jnp.stack(
        [
            own,
            plus[:, :-1],
            -minus[:, 1:],
            right[..., :-1],
            -left[..., 1:],
            time_step * inner,
            inner,
            jnp.zeros_like(inner),
        ],
        axis=2,
    )


def with_halo(value, sides, width):
    for axis, dim in sides:
        size, length = (lax.axis_size(axis), value.shape[dim])
        up = [(i, (i + 1) % size) for i in range(size - 1)]
        down = [(j, i) for i, j in up]
        last = lax.slice_in_dim(value, length - width, length, axis=dim)
        initial = lax.slice_in_dim(value, 0, width, axis=dim)
        before = lax.ppermute(last, axis, up)
        after = lax.ppermute(initial, axis, down)
        value = jnp.concatenate([before, value, after], axis=dim)
    return value


def as_sent(value):
    return jax.tree.map(lambda a: a.astype(jnp.bfloat16) if a.dtype == jnp.float32 else a, value)


def face_flux(behind_cells, ahead_cells, flow_speed, opened):
    moved = jnp.maximum(flow_speed, 0.0) * behind_cells + jnp.minimum(flow_speed, 0.0) * ahead_cells
    return opened * (moved - diffusion * (ahead_cells - behind_cells))


def plain_network(inputs, in_weight, in_bias, mid_weight, mid_bias, out_weight):
    kinds, depth, rows, cols = inputs.shape
    cells = depth * rows * cols
    turns = math.gcd(cells, 8)
    blocked = jnp.moveaxis(inputs.reshape(kinds, turns, cells // turns), 1, 0)

    def one_block(cell_block):
        first_hidden = (
            jnp.einsum("tn,th->nh", cell_block, in_weight, preferred_element_type=jnp.float32)
            + in_bias
        )
        first_hidden = jax.nn.silu(first_hidden).astype(jnp.bfloat16)
        second_hidden = (
            jnp.einsum("nh,hk->nk", first_hidden, mid_weight, preferred_element_type=jnp.float32)
            + mid_bias
        )
        second_hidden = jax.nn.silu(second_hidden).astype(jnp.bfloat16)
        return jnp.einsum(
            "nh,ht->tn", second_hidden, out_weight, preferred_element_type=jnp.float32
        ).astype(jnp.bfloat16)

    result = jnp.moveaxis(lax.map(one_block, blocked), 0, 1)
    return result.reshape(result.shape[0], depth, rows, cols)


def plain_body(
    tracers,
    east_speed,
    north_speed,
    land_mask,
    bottom_level,
    in_weight,
    in_bias,
    mid_weight,
    mid_bias,
    out_weight,
):
    levels = east_speed.shape[0]
    depth = jnp.arange(levels, dtype=jnp.int32)[:, None, None]
    wet_cells = ((land_mask[None] == 1) & (depth < bottom_level[None])).astype(jnp.float32)
    geometry = with_halo(
        jnp.stack([east_speed, wet_cells]).astype(jnp.bfloat16), (("tile", 2),), 1
    ).astype(jnp.float32)
    flow_x = geometry[0, :, :-1]
    wet_x = geometry[1]
    opened_x = wet_x[:, :-1] * wet_x[:, 1:]
    flow_y = jnp.pad(north_speed, ((0, 0), (0, 0), (1, 0)))
    wet_y = jnp.pad(wet_cells, ((0, 0), (0, 0), (1, 1)))
    opened_y = wet_y[..., :-1] * wet_y[..., 1:]
    field = tracers
    for step in range(STEPS):
        padded = with_halo(as_sent(field), (("tile", 2),), 1).astype(field.dtype)
        inputs = field.astype(jnp.bfloat16)
        local_sources = plain_network(
            lax.all_to_all(inputs, "tracer", split_axis=2, concat_axis=0, tiled=True),
            in_weight,
            in_bias,
            mid_weight,
            mid_bias,
            out_weight,
        )
        sources = lax.all_to_all(local_sources, "tracer", split_axis=0, concat_axis=2, tiled=True)
        x_flux = face_flux(padded[:, :, :-1], padded[:, :, 1:], flow_x, opened_x)
        cells_y = jnp.pad(field, ((0, 0), (0, 0), (0, 0), (1, 1)))
        y_flux = face_flux(cells_y[..., :-1], cells_y[..., 1:], flow_y, opened_y)
        tendency = x_flux[:, :, :-1] - x_flux[:, :, 1:] + (y_flux[..., :-1] - y_flux[..., 1:])
        field = wet_cells[None] * (field + time_step * (tendency + sources.astype(jnp.float32)))
    return field


def split_parts(value, count):
    parts = []
    for _ in range(count):
        parts.append(value.astype(BF16))
        value = value - parts[-1].astype(F32)
    return parts


def body(
    tracers,
    east_speed,
    north_speed,
    land_mask,
    bottom_level,
    in_weight,
    in_bias,
    mid_weight,
    mid_bias,
    out_weight,
):
    arguments = (
        tracers,
        east_speed,
        north_speed,
        land_mask,
        bottom_level,
        in_weight,
        in_bias,
        mid_weight,
        mid_bias,
        out_weight,
    )
    kinds, levels, length, columns = tracers.shape
    tiles, group = lax.axis_size("tile"), lax.axis_size("tracer")
    halves = 2
    stacks = group // halves
    rows = length // halves
    own = lax.axis_index("tracer")
    half, stack = own // stacks, own % stacks
    all_kinds = kinds * group
    thin = levels - stacks
    parts = columns // 128

    sent, place = kernel_call(
        pack_kernel,
        [
            jax.ShapeDtypeStruct((halves, stacks, kinds, 2, rows, columns), BF16),
            jax.ShapeDtypeStruct((length, columns), F32),
        ],
        [
            pltpu.VMEM((length, columns), F32),
            pltpu.VMEM((length * 32, 2 * columns), BF16),
            pltpu.VMEM((2 * columns, columns), BF16),
            pltpu.VMEM((parts, kinds * thin * length, 128), F32),
            pltpu.VMEM((kinds, stacks * length, columns), F32),
            pltpu.VMEM((parts, kinds * stacks * length, 128), F32),
            pltpu.SemaphoreType.DMA((kinds * parts + 1,)),
        ],
        2 * length * columns * columns * (32 + 64),
        "pack",
        [HBM, None, None],
    )(tracers.reshape(kinds, levels * length, columns), land_mask, bottom_level)
    sent = sent.reshape(group, kinds, 2, rows, columns)
    cells = lax.all_to_all(sent, "tracer", split_axis=0, concat_axis=0, tiled=True)
    cells = cells.reshape(all_kinds, 2, rows, columns)

    east_speed, north_speed, land_mask, sent = lax.optimization_barrier(
        (east_speed, north_speed, land_mask, sent)
    )
    depth = jnp.where(land_mask == 1, bottom_level, 0).astype(F32)
    level_list = [stack, stacks + stack, 2 * stacks + (stack + stacks // 2) % stacks]

    side, position = stack // (stacks // 2), stack % (stacks // 2)

    def own_levels(value):
        value = value.reshape(2 * levels // stacks, stacks // 2, length, columns)
        value = lax.dynamic_slice_in_dim(value, position, 1, 1)[:, 0]
        return jnp.where(
            side == 0,
            jnp.stack([value[0], value[2], value[5]]),
            jnp.stack([value[1], value[3], value[4]]),
        )

    geometry = [own_levels(east_speed), own_levels(north_speed), depth[None], place[None]]

    def at(tile, part, position):
        return tile * group + part * stacks + position

    across, within = [], []
    for position in range(stacks):
        for tile in range(tiles):
            within.append((at(tile, 0, position), at(tile, 1, position)))
            if tile + 1 < tiles:
                across.append((at(tile, 1, position), at(tile + 1, 0, position)))
    back = [(j, i) for i, j in across]
    axes = ("tile", "tracer")
    edge = jnp.concatenate(
        [lax.dynamic_slice_in_dim(value, half * (length - 2), 2, 1) for value in geometry], axis=0
    )
    arrived = lax.ppermute(edge, axes, across + back)
    arrived = [arrived[:3], arrived[3:6], arrived[6:7], arrived[7:8]]

    def widened(value, outside):
        return jnp.where(
            half == 0,
            jnp.concatenate([outside, value[:, : rows + 2]], axis=1),
            jnp.concatenate([value[:, rows - 2 :], outside], axis=1),
        )

    east, north, wide_depth, wide_place = [widened(*pair) for pair in zip(geometry, arrived)]
    factors = factors_of(east, north, wide_depth[0], jnp.stack(level_list).astype(F32)).reshape(
        3 * (rows + 2), 8, columns
    )

    level = jnp.arange(levels, dtype=jnp.int32).astype(F32)
    count = jnp.sum((level[:, None, None] < depth[None]).astype(F32), axis=2)
    deep = jnp.roll(count[2 * stacks :], -(stacks // 2), axis=0)
    deep = jnp.flip(deep.reshape(stacks, length // 2, 2), axis=2).reshape(stacks, length)
    fullest = count[stacks : 2 * stacks] + deep
    fullest, cells = lax.optimization_barrier((fullest, cells))

    in_parts = jnp.stack(split_parts(0.5 * in_bias, 3) + [jnp.zeros(in_bias.shape, BF16)] * 13, axis=1)
    weights = (
        jnp.concatenate([(0.5 * in_weight.astype(F32)).astype(BF16).T, in_parts], axis=1),
        (0.5 * mid_weight.astype(F32)).astype(BF16).T,
        jnp.broadcast_to(0.5 * mid_bias[:, None], mid_bias.shape + (128,)),
        out_weight.T,
    )

    hidden = in_weight.shape[1]
    pieces = 2 * rows
    per_piece = 2 * columns * hidden * (hidden + 2 * all_kinds)
    turned, first, last = kernel_call(
        functools.partial(turn_kernel, rows),
        [
            jax.ShapeDtypeStruct((pieces, all_kinds, columns), BF16),
            jax.ShapeDtypeStruct((4, all_kinds, columns), BF16),
            jax.ShapeDtypeStruct((4, all_kinds, columns), BF16),
        ],
        [pltpu.VMEM((parts, all_kinds * rows, 128), F32)],
        1_000_000,
        "turn",
    )(cells)
    top = lax.ppermute(last, axes, within + across)
    bottom = lax.ppermute(first, axes, [(j, i) for i, j in within] + back)
    partial, spread, table = kernel_call(
        functools.partial(source_kernel, rows),
        [
            jax.ShapeDtypeStruct((3 * rows, all_kinds, columns), F32),
            jax.ShapeDtypeStruct((2 * rows, all_kinds, columns), BF16),
            jax.ShapeDtypeStruct((rows + 4, columns, columns), BF16),
        ],
        [pltpu.VMEM((rows // 2, all_kinds, 4 * columns), BF16)],
        pieces * per_piece,
        "sources",
    )(turned, wide_place[0], factors, *weights)
    change = kernel_call(
        functools.partial(step_kernel, rows),
        jax.ShapeDtypeStruct(cells.shape, BF16),
        [
            pltpu.VMEM((3 * (rows + 2), all_kinds, columns), F32),
            pltpu.VMEM((rows, all_kinds, columns), BF16),
            pltpu.VMEM((rows // 2, all_kinds, 4 * columns), BF16),
            pltpu.VMEM((parts, 2 * rows * all_kinds, 128), F32),
        ],
        pieces * per_piece,
        "steps",
    )(turned, spread, partial, top, bottom, table, factors, *weights)

    fullest, change = lax.optimization_barrier((fullest, change))
    for step in (1, tiles // 4):
        others = []
        for times in (1, 2, 3):
            pairs = [(tile, tile ^ (step * times)) for tile in range(tiles)]
            others.append(lax.ppermute(fullest, "tile", pairs))
        fullest = functools.reduce(jnp.maximum, others, fullest)
    excess = jnp.max(fullest) > columns

    change = change.reshape(group, kinds, 2, rows, columns)
    change = lax.all_to_all(change, "tracer", split_axis=0, concat_axis=0, tiled=True)
    change = change.reshape(halves, stacks, kinds, 2, rows, columns)

    def finish(change, place, arguments):
        return kernel_call(
            finish_kernel,
            jax.ShapeDtypeStruct(tracers.shape, F32),
            [
                pltpu.VMEM((parts, group * kinds * rows, 128), F32),
                pltpu.VMEM((parts, kinds * thin * length, 128), F32),
                pltpu.VMEM(tracers.shape, F32),
                pltpu.SemaphoreType.DMA((kinds,)),
                pltpu.SemaphoreType.DMA((kinds * levels // stacks,)),
            ],
            2 * length * columns * columns * 32,
            "finish",
            [HBM, None, None, None, None],
            [HBM],
            memory=63,
        )(arguments[0], change, place, arguments[3], arguments[4])

    def in_full(change, place, arguments):
        return plain_body(*arguments)

    return lax.cond(excess, in_full, finish, change, place, arguments)


def solution(mesh):
    return jax.shard_map(
        body,
        mesh=mesh,
        in_specs=(
            P("tracer", None, "tile", None),
            P(None, "tile", None),
            P(None, "tile", None),
            P("tile", None),
            P("tile", None),
            P(),
            P(),
            P(),
            P(),
            P(),
        ),
        out_specs=P("tracer", None, "tile", None),
        check_vma=False,
    )
```

```python
import functools
import math

import jax
import jax.numpy as jnp
from jax import lax
from jax.experimental import pallas as pl
from jax.experimental.pallas import tpu as pltpu
from jax.sharding import PartitionSpec as P

STEPS = 2
diffusion = 0.2
time_step = 0.2
GROUP = 4

BF16 = jnp.bfloat16
F32 = jnp.float32


def silu_of_half(half):
    return (half + half * jnp.tanh(half)).astype(BF16)


def network(cells, in_weight, mid_weight, mid_bias, out_weight):
    lanes = cells.shape[1]
    cells = jnp.concatenate([cells, jnp.ones((16, lanes), BF16)], axis=0)
    hidden = silu_of_half(jnp.dot(in_weight, cells, preferred_element_type=F32))
    hidden = jnp.dot(mid_weight, hidden, preferred_element_type=F32)
    hidden = silu_of_half(hidden + jnp.concatenate([mid_bias] * (lanes // 128), axis=1))
    return jnp.dot(out_weight, hidden, preferred_element_type=F32)


def turn_kernel(rows, x_ref, turned_ref, first_ref, last_ref, scratch):
    kinds, levels = x_ref.shape[:2]
    for level in range(levels):
        for part in range(scratch.shape[0]):
            block = x_ref[:, level, :, part * 128 : (part + 1) * 128]
            scratch[part] = block.astype(F32).reshape(kinds * rows, 128)
        for row in range(rows):
            picked = [scratch[part, pl.ds(row, kinds, stride=rows), :] for part in range(scratch.shape[0])]
            piece = jnp.concatenate(picked, axis=1).astype(BF16)
            turned_ref[level * rows + row] = piece
            if row < 2:
                first_ref[level * 2 + row] = piece
            if row >= rows - 2:
                last_ref[level * 2 + row - rows + 2] = piece


def advance(here, above, below, sources, factors, from_above, from_below):
    width = here.shape[1]
    west = pltpu.roll(here, 1, 1)
    east = pltpu.roll(here, width - 1, 1)
    result = factors[0:1] * here + from_above * above + from_below * below
    return result + factors[3:4] * west + factors[4:5] * east + factors[5:6] * sources


def nt(rows, table):
    return lax.dot_general(rows, table, (((1,), (1,)), ((), ())), preferred_element_type=F32)


def nn(rows, table):
    return jnp.dot(rows, table, preferred_element_type=F32)


def one_hot(place):
    width = place.shape[1]
    slots = lax.broadcasted_iota(jnp.int32, (width, width), 0).astype(F32)
    return jnp.where(slots == place, 1.0, 0.0).astype(BF16)


def halves_of(ref, start, size, stride):
    return jnp.concatenate(
        [ref[part, pl.ds(start, size, stride=stride), :] for part in range(ref.shape[0])], axis=1
    )


def put_halves(ref, start, size, stride, value):
    for part in range(ref.shape[0]):
        ref[part, pl.ds(start, size, stride=stride), :] = value[:, part * 128 : (part + 1) * 128]


def pack_kernel(
    x_ref,
    land_hbm,
    bottom_hbm,
    sent_hbm,
    place_ref,
    depth_ref,
    counts,
    table,
    held,
    plain,
    packed,
    land_ref,
    bottom_ref,
    sent_ref,
    arrivals,
    leaving,
):
    kinds, _, width = x_ref.shape
    length = land_ref.shape[0]
    halves, stacks, _, _, rows, _ = sent_ref.shape
    levels = x_ref.shape[1] // length
    thin = levels - stacks
    parts = held.shape[0]
    copies = []
    for kind in range(kinds):
        for part in range(parts):
            copies.append(
                pltpu.make_async_copy(
                    x_ref.at[kind, pl.ds(stacks * length, thin * length), pl.ds(part * 128, 128)],
                    held.at[part, pl.ds(kind * thin * length, thin * length)],
                    arrivals.at[len(copies)],
                )
            )
    copies.append(
        pltpu.make_async_copy(x_ref.at[:, pl.ds(0, stacks * length)], plain, arrivals.at[len(copies)])
    )
    masks = [
        pltpu.make_async_copy(land_hbm, land_ref, arrivals.at[len(copies)]),
        pltpu.make_async_copy(bottom_hbm, bottom_ref, arrivals.at[len(copies) + 1]),
    ]
    for copy in masks + copies:
        copy.start()
    for copy in masks:
        copy.wait()
    depth_ref[...] = jnp.where(land_ref[...] == 1, bottom_ref[...], 0).astype(F32)
    bins = 32
    value = lax.broadcasted_iota(jnp.int32, (bins, width), 0).astype(F32)
    for row in range(length):
        depth = depth_ref[row : row + 1]
        counts[row * bins : (row + 1) * bins, :width] = jnp.where(depth == value, 1.0, 0.0).astype(BF16)
        counts[row * bins : (row + 1) * bins, width:] = jnp.where(depth > value, 1.0, 0.0).astype(BF16)
    before = lax.broadcasted_iota(jnp.int32, (width, width), 0)
    after = lax.broadcasted_iota(jnp.int32, (width, width), 1)
    table[:width] = jnp.where(before < after, 1.0, 0.0).astype(BF16)
    table[width:] = jnp.ones((width, width), BF16)
    ranks = nn(counts[...], table[...])
    for row in range(length):
        here = jnp.where(depth_ref[row : row + 1] == value, ranks[row * bins : (row + 1) * bins], 0.0)
        place = jnp.sum(here, axis=0, keepdims=True)
        place_ref[row : row + 1] = place if row % 2 == 0 else (width - 1.0) - place

    for copy in copies:
        copy.wait()
    sent = []

    def send(half, kind, slot):
        block = (half, slice(None), kind, slot)
        sent.append(
            pltpu.make_async_copy(sent_ref.at[block], sent_hbm.at[block], leaving.at[len(sent)])
        )
        sent[-1].start()

    for half in range(halves):
        inside = slice(half * rows, (half + 1) * rows)
        for kind in range(kinds):
            block = plain[kind].reshape(stacks, length, width)
            sent_ref[half, :, kind, 0] = block[:, inside].astype(BF16)
            send(half, kind, 0)
    level = stacks + lax.broadcasted_iota(jnp.int32, (thin, width), 0).astype(F32)

    def body(i, _):
        sorted_rows = []
        for k in range(2):
            row = 2 * i + k
            wet = level < depth_ref[pl.ds(row, 1)]
            cells = [
                jnp.where(wet, halves_of(held, kind * thin * length + row, thin, length), 0.0).astype(BF16)
                for kind in range(kinds)
            ]
            sorted_rows.append(nt(jnp.concatenate(cells, axis=0), one_hot(place_ref[pl.ds(row, 1)])))
        for k in range(2):
            for kind in range(kinds):
                at = kind * thin
                deep = sorted_rows[1 - k][at + stacks : at + 2 * stacks]
                value = sorted_rows[k][at : at + stacks] + pltpu.roll(deep, stacks // 2, 0)
                put_halves(packed, kind * stacks * length + 2 * i + k, stacks, length, value)
        return 0

    lax.fori_loop(0, length // 2, body, 0, unroll=8)
    for half in range(halves):
        inside = slice(half * rows, (half + 1) * rows)
        for kind in range(kinds):
            for part in range(packed.shape[0]):
                at = kind * stacks * length
                block = packed[part, at : at + stacks * length].reshape(stacks, length, 128)
                sent_ref[half, :, kind, 1, :, part * 128 : (part + 1) * 128] = block[:, inside].astype(BF16)
            send(half, kind, 1)
    for copy in sent:
        copy.wait()


def finish_kernel(
    x_ref, arrived_ref, place_ref, land_ref, bottom_ref, result_ref, held, spread, field, arrivals, leaving
):
    kinds, levels, length, width = x_ref.shape
    copies = [pltpu.make_async_copy(x_ref.at[kind], field.at[kind], arrivals.at[kind]) for kind in range(kinds)]
    for copy in copies:
        copy.start()
    halves, stacks, _, _, rows, _ = arrived_ref.shape
    thin = levels - stacks
    each = stacks * kinds * rows
    for half in range(halves):
        for part in range(held.shape[0]):
            block = arrived_ref[half, :, :, 1, :, part * 128 : (part + 1) * 128]
            held[part, half * each : (half + 1) * each] = block.astype(F32).reshape(each, 128)

    def body(i, _):
        half = i // (rows // 2)
        row = 2 * i - half * rows
        cells = []
        for k in range(2):
            for kind in range(kinds):
                cells.append(halves_of(held, half * each + kind * rows + row + k, stacks, kinds * rows))
        cells = jnp.concatenate(cells, axis=0).astype(BF16)
        for k in range(2):
            value = nn(cells, one_hot(place_ref[pl.ds(2 * i + k, 1)]))
            for kind in range(kinds):
                near = (k * kinds + kind) * stacks
                other = ((1 - k) * kinds + kind) * stacks
                at = kind * thin * length + 2 * i + k
                put_halves(spread, at, stacks, length, value[near : near + stacks])
                deep = pltpu.roll(value[other : other + stacks], stacks // 2, 0)
                put_halves(spread, at + stacks * length, stacks, length, deep)
        return 0

    lax.fori_loop(0, length // 2, body, 0, unroll=8)
    depth = jnp.where(land_ref[...] == 1, bottom_ref[...], 0)
    sent = []
    for kind in range(kinds):
        copies[kind].wait()
        for level in range(levels):
            if level < stacks:
                change = jnp.concatenate(
                    [arrived_ref[half, level, kind, 0] for half in range(halves)], axis=0
                ).astype(F32)
            else:
                at = (kind * thin + level - stacks) * length
                change = jnp.concatenate(
                    [spread[part, at : at + length] for part in range(spread.shape[0])], axis=1
                )
            field[kind, level] = jnp.where(level < depth, field[kind, level] + change, 0.0)
            if level % stacks == stacks - 1:
                block = pl.ds(level + 1 - stacks, stacks)
                sent.append(
                    pltpu.make_async_copy(
                        field.at[kind, block], result_ref.at[kind, block], leaving.at[len(sent)]
                    )
                )
                sent[-1].start()
    for copy in sent:
        copy.wait()


def source_kernel(
    rows,
    cells_ref,
    place_ref,
    factors_ref,
    in_ref,
    mid_ref,
    bias_ref,
    out_ref,
    middle_ref,
    spread_ref,
    table_ref,
    held,
):
    _, kinds, width = cells_ref.shape
    ahead = rows + 2
    weights = (in_ref, mid_ref, bias_ref, out_ref)

    def cell(level, row):
        if level == 0:
            return cells_ref[row]
        return spread_ref[(level - 1) * rows + row]

    def spread_out(i):
        row = 2 * i
        cells = jnp.concatenate([cells_ref[rows + row], cells_ref[rows + row + 1]], axis=0)
        for k in range(2):
            table = one_hot(place_ref[row + 2 + k : row + 3 + k])
            table_ref[row + 2 + k] = table
            value = nn(cells, table).astype(BF16)
            spread_ref[row + k] = value[k * kinds : (k + 1) * kinds]
            spread_ref[rows + row + k] = value[(1 - k) * kinds : (2 - k) * kinds]

    def sources(i):
        row = 2 * i
        cells = [cells_ref[row], cells_ref[row + 1], cells_ref[rows + row], cells_ref[rows + row + 1]]
        result = network(jnp.concatenate(cells, axis=1), *[ref[...] for ref in weights])
        held[i] = result.astype(BF16)

    def move(i):
        row = 2 * i
        result = held[i]
        packed = jnp.concatenate(
            [result[:, 2 * width : 3 * width], result[:, 3 * width :]], axis=0
        )
        for k in range(2):
            value = nn(packed, table_ref[row + 2 + k])
            pieces = [
                result[:, k * width : (k + 1) * width].astype(F32),
                value[k * kinds : (k + 1) * kinds],
                value[(1 - k) * kinds : (2 - k) * kinds],
            ]
            for level in range(3):
                factors = factors_ref[level * ahead + row + 1 + k]
                above, below = factors[1:2], factors[2:3]
                if k == 0:
                    above = jnp.where(row > 0, above, 0.0)
                else:
                    below = jnp.where(row + 2 < rows, below, 0.0)
                middle_ref[level * rows + row + k] = advance(
                    cell(level, row + k).astype(F32),
                    cell(level, jnp.maximum(row + k - 1, 0)).astype(F32),
                    cell(level, jnp.minimum(row + k + 1, rows - 1)).astype(F32),
                    pieces[level],
                    factors,
                    above,
                    below,
                )

    def body(i, _):
        move(i - 1)
        sources(i)
        return 0

    for i in range(rows // 2):
        spread_out(i)
    for row in (0, 1, rows + 2, rows + 3):
        table_ref[row] = one_hot(place_ref[row : row + 1])
    sources(0)
    lax.fori_loop(1, rows // 2, body, 0)
    move(rows // 2 - 1)


def step_kernel(
    rows,
    cells_ref,
    spread_ref,
    partial_ref,
    top_ref,
    bottom_ref,
    table_ref,
    factors_ref,
    in_ref,
    mid_ref,
    bias_ref,
    out_ref,
    change_ref,
    middle,
    packed,
    held,
    scratch,
):
    _, kinds, width = cells_ref.shape
    ahead = rows + 2
    weights = (in_ref, mid_ref, bias_ref, out_ref)

    def run(cells):
        return network(jnp.concatenate(cells, axis=1), *[ref[...] for ref in weights]).astype(BF16)

    for level in range(3):
        for row in range(1, rows - 1):
            middle[level * ahead + 1 + row] = partial_ref[level * rows + row]


    def put_together(row, thin):
        values = [nt(thin[k], table_ref[row + 2 + k]) for k in range(2)]
        return [values[k][:kinds] + values[1 - k][kinds:] for k in range(2)]

    def pack(i):
        row = 2 * i
        thin = [
            jnp.concatenate(
                [middle[level * ahead + 1 + row + k].astype(BF16) for level in (1, 2)], axis=0
            )
            for k in range(2)
        ]
        values = put_together(row, thin)
        for k in range(2):
            packed[row + k] = values[k].astype(BF16)

    def sources_of(i):
        row = 2 * i
        cells = [middle[1 + row + k].astype(BF16) for k in range(2)]
        held[i] = run(cells + [packed[row], packed[row + 1]])

    def move(i):
        row = 2 * i
        result = held[i]
        thin_sources = jnp.concatenate(
            [result[:, 2 * width : 3 * width], result[:, 3 * width :]], axis=0
        )
        changes = []
        for k in range(2):
            value = nn(thin_sources, table_ref[row + 2 + k])
            pieces = [
                result[:, k * width : (k + 1) * width].astype(F32),
                value[k * kinds : (k + 1) * kinds],
                value[(1 - k) * kinds : (2 - k) * kinds],
            ]
            for level in range(3):
                at = level * ahead + 1 + row + k
                factors = factors_ref[at]
                value = advance(
                    middle[at],
                    middle[at - 1],
                    middle[at + 1],
                    pieces[level],
                    factors,
                    factors[1:2],
                    factors[2:3],
                )
                if level == 0:
                    first = cells_ref[row + k]
                else:
                    first = spread_ref[(level - 1) * rows + row + k]
                changes.append(value - factors[6:7] * first.astype(F32))
        thin = [
            jnp.concatenate([changes[3 * k + 1].astype(BF16), changes[3 * k + 2].astype(BF16)], axis=0)
            for k in range(2)
        ]
        values = put_together(row, thin)
        for k in range(2):
            put_halves(scratch, row + k, kinds, rows, changes[3 * k])
            put_halves(scratch, rows * kinds + row + k, kinds, rows, values[k])

    def turn(i):
        return (i + 1) % (rows // 2)

    def body(i, _):
        move(turn(i - 1))
        sources_of(turn(i))
        return 0

    for i in range(1, rows // 2 - 1):
        pack(i)
    edges = [
        [top_ref[1], top_ref[2], top_ref[3]],
        [bottom_ref[0], bottom_ref[2], bottom_ref[3]],
    ]
    result = run(edges[0] + edges[1])
    for k in range(2):
        packed_cells = jnp.concatenate(edges[k][1:], axis=0)
        at = 3 * k * width
        packed_sources = jnp.concatenate(
            [result[:, at + width : at + 2 * width], result[:, at + 2 * width : at + 3 * width]], axis=0
        )
        near = nn(jnp.concatenate([packed_cells, packed_sources], axis=0), table_ref[[1, rows + 2][k]])
        far = nn(packed_cells, table_ref[[0, rows + 3][k]])
        near_at = [[1, 0], [0, 1]][k]
        far_at = [[0, 1], [1, 0]][k]
        for level in range(3):
            inside = level * rows + k * (rows - 1)
            if level == 0:
                own = edges[k][0].astype(F32)
                other = (top_ref[0] if k == 0 else bottom_ref[1]).astype(F32)
                sources = result[:, at : at + width].astype(F32)
                inner = cells_ref[k * (rows - 1)].astype(F32)
            else:
                place = near_at[level - 1] * kinds
                own = near[place : place + kinds]
                sources = near[2 * kinds + place : 3 * kinds + place]
                place = far_at[level - 1] * kinds
                other = far[place : place + kinds]
                inner = spread_ref[(level - 1) * rows + k * (rows - 1)].astype(F32)
            row = level * ahead + k * (ahead - 1)
            factors = factors_ref[row]
            middle[row] = advance(
                own,
                other if k == 0 else inner,
                inner if k == 0 else other,
                sources,
                factors,
                factors[1:2],
                factors[2:3],
            )
            row = level * ahead + 1 + k * (rows - 1)
            middle[row] = partial_ref[inside] + factors_ref[row][1 + k : 2 + k] * own
    sources_of(1)
    pack(0)
    pack(rows // 2 - 1)
    lax.fori_loop(1, rows // 2, body, 0, unroll=True)
    move(0)
    for level in range(2):
        for part in range(scratch.shape[0]):
            block = scratch[part, level * rows * kinds : (level + 1) * rows * kinds, :]
            change_ref[:, level, :, part * 128 : (part + 1) * 128] = block.reshape(kinds, rows, 128).astype(BF16)


HBM = pltpu.HBM


def kernel_call(kernel, outs, scratch, flops, name, places=None, result_places=None, memory=32):
    def specs(given):
        return [pl.BlockSpec(memory_space=place or pltpu.VMEM) for place in given]

    spaces = {} if places is None else {"in_specs": specs(places)}
    if result_places is not None:
        given = specs(result_places)
        spaces["out_specs"] = given if isinstance(outs, list) else given[0]
    return pl.pallas_call(
        kernel,
        out_shape=outs,
        **spaces,
        scratch_shapes=scratch,
        cost_estimate=pl.CostEstimate(flops=flops, bytes_accessed=4_000_000, transcendentals=0),
        compiler_params=pltpu.CompilerParams(vmem_limit_bytes=memory * 2**20),
        name=name,
    )


def factors_of(east, north, depth, level):
    wet = (level[:, None, None] < depth[None]).astype(F32)
    opened = time_step * wet[:, :-1] * wet[:, 1:]
    plus = opened * (jnp.maximum(east[:, :-1], 0.0) + diffusion)
    minus = opened * (jnp.minimum(east[:, :-1], 0.0) - diffusion)
    inner = wet[:, 1:-1]
    flow = jnp.pad(north[:, 1:-1], ((0, 0), (0, 0), (1, 0)))
    sides = jnp.pad(inner, ((0, 0), (0, 0), (1, 1)))
    opened = time_step * sides[..., :-1] * sides[..., 1:]
    right = opened * (jnp.maximum(flow, 0.0) + diffusion)
    left = opened * (jnp.minimum(flow, 0.0) - diffusion)
    own = inner + (minus[:, :-1] - plus[:, 1:]) + (left[..., :-1] - right[..., 1:])
    return jnp.stack(
        [
            own,
            plus[:, :-1],
            -minus[:, 1:],
            right[..., :-1],
            -left[..., 1:],
            time_step * inner,
            inner,
            jnp.zeros_like(inner),
        ],
        axis=2,
    )


def with_halo(value, sides, width):
    for axis, dim in sides:
        size, length = (lax.axis_size(axis), value.shape[dim])
        up = [(i, (i + 1) % size) for i in range(size - 1)]
        down = [(j, i) for i, j in up]
        last = lax.slice_in_dim(value, length - width, length, axis=dim)
        initial = lax.slice_in_dim(value, 0, width, axis=dim)
        before = lax.ppermute(last, axis, up)
        after = lax.ppermute(initial, axis, down)
        value = jnp.concatenate([before, value, after], axis=dim)
    return value


def as_sent(value):
    return jax.tree.map(lambda a: a.astype(jnp.bfloat16) if a.dtype == jnp.float32 else a, value)


def face_flux(behind_cells, ahead_cells, flow_speed, opened):
    moved = jnp.maximum(flow_speed, 0.0) * behind_cells + jnp.minimum(flow_speed, 0.0) * ahead_cells
    return opened * (moved - diffusion * (ahead_cells - behind_cells))


def plain_network(inputs, in_weight, in_bias, mid_weight, mid_bias, out_weight):
    kinds, depth, rows, cols = inputs.shape
    cells = depth * rows * cols
    turns = math.gcd(cells, 8)
    blocked = jnp.moveaxis(inputs.reshape(kinds, turns, cells // turns), 1, 0)

    def one_block(cell_block):
        first_hidden = (
            jnp.einsum("tn,th->nh", cell_block, in_weight, preferred_element_type=jnp.float32)
            + in_bias
        )
        first_hidden = jax.nn.silu(first_hidden).astype(jnp.bfloat16)
        second_hidden = (
            jnp.einsum("nh,hk->nk", first_hidden, mid_weight, preferred_element_type=jnp.float32)
            + mid_bias
        )
        second_hidden = jax.nn.silu(second_hidden).astype(jnp.bfloat16)
        return jnp.einsum(
            "nh,ht->tn", second_hidden, out_weight, preferred_element_type=jnp.float32
        ).astype(jnp.bfloat16)

    result = jnp.moveaxis(lax.map(one_block, blocked), 0, 1)
    return result.reshape(result.shape[0], depth, rows, cols)


def plain_body(
    tracers,
    east_speed,
    north_speed,
    land_mask,
    bottom_level,
    in_weight,
    in_bias,
    mid_weight,
    mid_bias,
    out_weight,
):
    levels = east_speed.shape[0]
    depth = jnp.arange(levels, dtype=jnp.int32)[:, None, None]
    wet_cells = ((land_mask[None] == 1) & (depth < bottom_level[None])).astype(jnp.float32)
    geometry = with_halo(
        jnp.stack([east_speed, wet_cells]).astype(jnp.bfloat16), (("tile", 2),), 1
    ).astype(jnp.float32)
    flow_x = geometry[0, :, :-1]
    wet_x = geometry[1]
    opened_x = wet_x[:, :-1] * wet_x[:, 1:]
    flow_y = jnp.pad(north_speed, ((0, 0), (0, 0), (1, 0)))
    wet_y = jnp.pad(wet_cells, ((0, 0), (0, 0), (1, 1)))
    opened_y = wet_y[..., :-1] * wet_y[..., 1:]
    field = tracers
    for step in range(STEPS):
        padded = with_halo(as_sent(field), (("tile", 2),), 1).astype(field.dtype)
        inputs = field.astype(jnp.bfloat16)
        local_sources = plain_network(
            lax.all_to_all(inputs, "tracer", split_axis=2, concat_axis=0, tiled=True),
            in_weight,
            in_bias,
            mid_weight,
            mid_bias,
            out_weight,
        )
        sources = lax.all_to_all(local_sources, "tracer", split_axis=0, concat_axis=2, tiled=True)
        x_flux = face_flux(padded[:, :, :-1], padded[:, :, 1:], flow_x, opened_x)
        cells_y = jnp.pad(field, ((0, 0), (0, 0), (0, 0), (1, 1)))
        y_flux = face_flux(cells_y[..., :-1], cells_y[..., 1:], flow_y, opened_y)
        tendency = x_flux[:, :, :-1] - x_flux[:, :, 1:] + (y_flux[..., :-1] - y_flux[..., 1:])
        field = wet_cells[None] * (field + time_step * (tendency + sources.astype(jnp.float32)))
    return field


def split_parts(value, count):
    parts = []
    for _ in range(count):
        parts.append(value.astype(BF16))
        value = value - parts[-1].astype(F32)
    return parts


def body(
    tracers,
    east_speed,
    north_speed,
    land_mask,
    bottom_level,
    in_weight,
    in_bias,
    mid_weight,
    mid_bias,
    out_weight,
):
    arguments = (
        tracers,
        east_speed,
        north_speed,
        land_mask,
        bottom_level,
        in_weight,
        in_bias,
        mid_weight,
        mid_bias,
        out_weight,
    )
    kinds, levels, length, columns = tracers.shape
    tiles, group = lax.axis_size("tile"), lax.axis_size("tracer")
    halves = 2
    stacks = group // halves
    rows = length // halves
    own = lax.axis_index("tracer")
    half, stack = own // stacks, own % stacks
    all_kinds = kinds * group
    thin = levels - stacks
    parts = columns // 128

    sent, place = kernel_call(
        pack_kernel,
        [
            jax.ShapeDtypeStruct((halves, stacks, kinds, 2, rows, columns), BF16),
            jax.ShapeDtypeStruct((length, columns), F32),
        ],
        [
            pltpu.VMEM((length, columns), F32),
            pltpu.VMEM((length * 32, 2 * columns), BF16),
            pltpu.VMEM((2 * columns, columns), BF16),
            pltpu.VMEM((parts, kinds * thin * length, 128), F32),
            pltpu.VMEM((kinds, stacks * length, columns), F32),
            pltpu.VMEM((parts, kinds * stacks * length, 128), F32),
            pltpu.VMEM((length, columns), jnp.int32),
            pltpu.VMEM((length, columns), jnp.int32),
            pltpu.VMEM((halves, stacks, kinds, 2, rows, columns), BF16),
            pltpu.SemaphoreType.DMA((kinds * parts + 3,)),
            pltpu.SemaphoreType.DMA((halves * kinds * 2,)),
        ],
        2 * length * columns * columns * (32 + 64),
        "pack",
        [HBM, HBM, HBM],
        [HBM, None],
    )(tracers.reshape(kinds, levels * length, columns), land_mask, bottom_level)
    sent = sent.reshape(group, kinds, 2, rows, columns)
    cells = lax.all_to_all(sent, "tracer", split_axis=0, concat_axis=0, tiled=True)
    cells = cells.reshape(all_kinds, 2, rows, columns)

    east_speed, north_speed, land_mask, sent = lax.optimization_barrier(
        (east_speed, north_speed, land_mask, sent)
    )
    depth = jnp.where(land_mask == 1, bottom_level, 0).astype(F32)
    level_list = [stack, stacks + stack, 2 * stacks + (stack + stacks // 2) % stacks]

    side, position = stack // (stacks // 2), stack % (stacks // 2)

    def own_levels(value):
        value = value.reshape(2 * levels // stacks, stacks // 2, length, columns)
        value = lax.dynamic_slice_in_dim(value, position, 1, 1)[:, 0]
        return jnp.where(
            side == 0,
            jnp.stack([value[0], value[2], value[5]]),
            jnp.stack([value[1], value[3], value[4]]),
        )

    geometry = [own_levels(east_speed), own_levels(north_speed), depth[None], place[None]]

    def at(tile, part, position):
        return tile * group + part * stacks + position

    across, within = [], []
    for position in range(stacks):
        for tile in range(tiles):
            within.append((at(tile, 0, position), at(tile, 1, position)))
            if tile + 1 < tiles:
                across.append((at(tile, 1, position), at(tile + 1, 0, position)))
    back = [(j, i) for i, j in across]
    axes = ("tile", "tracer")
    edge = jnp.concatenate(
        [lax.dynamic_slice_in_dim(value, half * (length - 2), 2, 1) for value in geometry], axis=0
    )
    arrived = lax.ppermute(edge, axes, across + back)
    arrived = [arrived[:3], arrived[3:6], arrived[6:7], arrived[7:8]]

    def widened(value, outside):
        return jnp.where(
            half == 0,
            jnp.concatenate([outside, value[:, : rows + 2]], axis=1),
            jnp.concatenate([value[:, rows - 2 :], outside], axis=1),
        )

    east, north, wide_depth, wide_place = [widened(*pair) for pair in zip(geometry, arrived)]
    factors = factors_of(east, north, wide_depth[0], jnp.stack(level_list).astype(F32)).reshape(
        3 * (rows + 2), 8, columns
    )

    level = jnp.arange(levels, dtype=jnp.int32).astype(F32)
    count = jnp.sum((level[:, None, None] < depth[None]).astype(F32), axis=2)
    deep = jnp.roll(count[2 * stacks :], -(stacks // 2), axis=0)
    deep = jnp.flip(deep.reshape(stacks, length // 2, 2), axis=2).reshape(stacks, length)
    fullest = count[stacks : 2 * stacks] + deep
    fullest, cells = lax.optimization_barrier((fullest, cells))

    in_parts = jnp.stack(split_parts(0.5 * in_bias, 3) + [jnp.zeros(in_bias.shape, BF16)] * 13, axis=1)
    weights = (
        jnp.concatenate([(0.5 * in_weight.astype(F32)).astype(BF16).T, in_parts], axis=1),
        (0.5 * mid_weight.astype(F32)).astype(BF16).T,
        jnp.broadcast_to(0.5 * mid_bias[:, None], mid_bias.shape + (128,)),
        out_weight.T,
    )

    hidden = in_weight.shape[1]
    pieces = 2 * rows
    per_piece = 2 * columns * hidden * (hidden + 2 * all_kinds)
    turned, first, last = kernel_call(
        functools.partial(turn_kernel, rows),
        [
            jax.ShapeDtypeStruct((pieces, all_kinds, columns), BF16),
            jax.ShapeDtypeStruct((4, all_kinds, columns), BF16),
            jax.ShapeDtypeStruct((4, all_kinds, columns), BF16),
        ],
        [pltpu.VMEM((parts, all_kinds * rows, 128), F32)],
        1_000_000,
        "turn",
    )(cells)
    top = lax.ppermute(last, axes, within + across)
    bottom = lax.ppermute(first, axes, [(j, i) for i, j in within] + back)
    partial, spread, table = kernel_call(
        functools.partial(source_kernel, rows),
        [
            jax.ShapeDtypeStruct((3 * rows, all_kinds, columns), F32),
            jax.ShapeDtypeStruct((2 * rows, all_kinds, columns), BF16),
            jax.ShapeDtypeStruct((rows + 4, columns, columns), BF16),
        ],
        [pltpu.VMEM((rows // 2, all_kinds, 4 * columns), BF16)],
        pieces * per_piece,
        "sources",
    )(turned, wide_place[0], factors, *weights)
    change = kernel_call(
        functools.partial(step_kernel, rows),
        jax.ShapeDtypeStruct(cells.shape, BF16),
        [
            pltpu.VMEM((3 * (rows + 2), all_kinds, columns), F32),
            pltpu.VMEM((rows, all_kinds, columns), BF16),
            pltpu.VMEM((rows // 2, all_kinds, 4 * columns), BF16),
            pltpu.VMEM((parts, 2 * rows * all_kinds, 128), F32),
        ],
        pieces * per_piece,
        "steps",
    )(turned, spread, partial, top, bottom, table, factors, *weights)

    fullest, change = lax.optimization_barrier((fullest, change))
    for step in (1, tiles // 4):
        others = []
        for times in (1, 2, 3):
            pairs = [(tile, tile ^ (step * times)) for tile in range(tiles)]
            others.append(lax.ppermute(fullest, "tile", pairs))
        fullest = functools.reduce(jnp.maximum, others, fullest)
    excess = jnp.max(fullest) > columns

    change = change.reshape(group, kinds, 2, rows, columns)
    change = lax.all_to_all(change, "tracer", split_axis=0, concat_axis=0, tiled=True)
    change = change.reshape(halves, stacks, kinds, 2, rows, columns)

    def finish(change, place, arguments):
        return kernel_call(
            finish_kernel,
            jax.ShapeDtypeStruct(tracers.shape, F32),
            [
                pltpu.VMEM((parts, group * kinds * rows, 128), F32),
                pltpu.VMEM((parts, kinds * thin * length, 128), F32),
                pltpu.VMEM(tracers.shape, F32),
                pltpu.SemaphoreType.DMA((kinds,)),
                pltpu.SemaphoreType.DMA((kinds * levels // stacks,)),
            ],
            2 * length * columns * columns * 32,
            "finish",
            [HBM, None, None, None, None],
            [HBM],
            memory=63,
        )(arguments[0], change, place, arguments[3], arguments[4])

    def in_full(change, place, arguments):
        return plain_body(*arguments)

    return lax.cond(excess, in_full, finish, change, place, arguments)


def solution(mesh):
    return jax.shard_map(
        body,
        mesh=mesh,
        in_specs=(
            P("tracer", None, "tile", None),
            P(None, "tile", None),
            P(None, "tile", None),
            P("tile", None),
            P("tile", None),
            P(),
            P(),
            P(),
            P(),
            P(),
        ),
        out_specs=P("tracer", None, "tile", None),
        check_vma=False,
    )
```

```python
import functools
import math

import jax
import jax.numpy as jnp
from jax import lax
from jax.experimental import pallas as pl
from jax.experimental.pallas import tpu as pltpu
from jax.sharding import PartitionSpec as P

STEPS = 2
diffusion = 0.2
time_step = 0.2
GROUP = 4

BF16 = jnp.bfloat16
F32 = jnp.float32


def silu_of_half(half):
    return (half + half * jnp.tanh(half)).astype(BF16)


def network(cells, in_weight, mid_weight, mid_bias, out_weight):
    lanes = cells.shape[1]
    cells = jnp.concatenate([cells, jnp.ones((16, lanes), BF16)], axis=0)
    hidden = silu_of_half(jnp.dot(in_weight, cells, preferred_element_type=F32))
    hidden = jnp.dot(mid_weight, hidden, preferred_element_type=F32)
    hidden = silu_of_half(hidden + jnp.concatenate([mid_bias] * (lanes // 128), axis=1))
    return jnp.dot(out_weight, hidden, preferred_element_type=F32)


def turn_kernel(rows, x_ref, turned_ref, first_ref, last_ref, scratch):
    kinds, levels = x_ref.shape[:2]
    for level in range(levels):
        for part in range(scratch.shape[0]):
            block = x_ref[:, level, :, part * 128 : (part + 1) * 128]
            scratch[part, : kinds * rows] = block.astype(F32).reshape(kinds * rows, 128)
        for row in range(rows):
            picked = [scratch[part, pl.ds(row, kinds, stride=rows), :] for part in range(scratch.shape[0])]
            piece = jnp.concatenate(picked, axis=1).astype(BF16)
            turned_ref[level * rows + row] = piece
            if row < 2:
                first_ref[level * 2 + row] = piece
            if row >= rows - 2:
                last_ref[level * 2 + row - rows + 2] = piece


def advance(here, above, below, sources, factors, from_above, from_below):
    width = here.shape[1]
    west = pltpu.roll(here, 1, 1)
    east = pltpu.roll(here, width - 1, 1)
    result = factors[0:1] * here + from_above * above + from_below * below
    return result + factors[3:4] * west + factors[4:5] * east + factors[5:6] * sources


def nt(rows, table):
    return lax.dot_general(rows, table, (((1,), (1,)), ((), ())), preferred_element_type=F32)


def nn(rows, table):
    return jnp.dot(rows, table, preferred_element_type=F32)


def one_hot(place):
    width = place.shape[1]
    slots = lax.broadcasted_iota(jnp.int32, (width, width), 0).astype(F32)
    return jnp.where(slots == place, 1.0, 0.0).astype(BF16)


def halves_of(ref, start, size, stride):
    return jnp.concatenate(
        [ref[part, pl.ds(start, size, stride=stride), :] for part in range(ref.shape[0])], axis=1
    )


def put_halves(ref, start, size, stride, value):
    for part in range(ref.shape[0]):
        ref[part, pl.ds(start, size, stride=stride), :] = value[:, part * 128 : (part + 1) * 128]


def pack_kernel(
    x_ref,
    land_hbm,
    bottom_hbm,
    sent_hbm,
    place_ref,
    depth_ref,
    counts,
    table,
    held,
    plain,
    packed,
    land_ref,
    bottom_ref,
    sent_ref,
    arrivals,
    leaving,
):
    kinds, _, width = x_ref.shape
    length = land_ref.shape[0]
    halves, stacks, _, _, rows, _ = sent_ref.shape
    levels = x_ref.shape[1] // length
    thin = levels - stacks
    parts = held.shape[0]
    copies = []
    for kind in range(kinds):
        for part in range(parts):
            copies.append(
                pltpu.make_async_copy(
                    x_ref.at[kind, pl.ds(stacks * length, thin * length), pl.ds(part * 128, 128)],
                    held.at[part, pl.ds(kind * thin * length, thin * length)],
                    arrivals.at[len(copies)],
                )
            )
    copies.append(
        pltpu.make_async_copy(x_ref.at[:, pl.ds(0, stacks * length)], plain, arrivals.at[len(copies)])
    )
    masks = [
        pltpu.make_async_copy(land_hbm, land_ref, arrivals.at[len(copies)]),
        pltpu.make_async_copy(bottom_hbm, bottom_ref, arrivals.at[len(copies) + 1]),
    ]
    for copy in masks + copies:
        copy.start()
    for copy in masks:
        copy.wait()
    depth_ref[...] = jnp.where(land_ref[...] == 1, bottom_ref[...], 0).astype(F32)
    bins = 32
    value = lax.broadcasted_iota(jnp.int32, (bins, width), 0).astype(F32)
    for row in range(length):
        depth = depth_ref[row : row + 1]
        counts[row * bins : (row + 1) * bins, :width] = jnp.where(depth == value, 1.0, 0.0).astype(BF16)
        counts[row * bins : (row + 1) * bins, width:] = jnp.where(depth > value, 1.0, 0.0).astype(BF16)
    before = lax.broadcasted_iota(jnp.int32, (width, width), 0)
    after = lax.broadcasted_iota(jnp.int32, (width, width), 1)
    table[:width] = jnp.where(before < after, 1.0, 0.0).astype(BF16)
    table[width:] = jnp.ones((width, width), BF16)
    ranks = nn(counts[...], table[...])
    for row in range(length):
        here = jnp.where(depth_ref[row : row + 1] == value, ranks[row * bins : (row + 1) * bins], 0.0)
        place = jnp.sum(here, axis=0, keepdims=True)
        place_ref[row : row + 1] = place if row % 2 == 0 else (width - 1.0) - place

    for copy in copies:
        copy.wait()
    sent = []

    def send(half, kind, slot):
        block = (half, slice(None), kind, slot)
        sent.append(
            pltpu.make_async_copy(sent_ref.at[block], sent_hbm.at[block], leaving.at[len(sent)])
        )
        sent[-1].start()

    for half in range(halves):
        inside = slice(half * rows, (half + 1) * rows)
        for kind in range(kinds):
            block = plain[kind].reshape(stacks, length, width)
            sent_ref[half, :, kind, 0] = block[:, inside].astype(BF16)
            send(half, kind, 0)
    level = stacks + lax.broadcasted_iota(jnp.int32, (thin, width), 0).astype(F32)

    def body(i, _):
        sorted_rows = []
        for k in range(2):
            row = 2 * i + k
            wet = level < depth_ref[pl.ds(row, 1)]
            cells = [
                jnp.where(wet, halves_of(held, kind * thin * length + row, thin, length), 0.0).astype(BF16)
                for kind in range(kinds)
            ]
            sorted_rows.append(nt(jnp.concatenate(cells, axis=0), one_hot(place_ref[pl.ds(row, 1)])))
        for k in range(2):
            for kind in range(kinds):
                at = kind * thin
                deep = sorted_rows[1 - k][at + stacks : at + 2 * stacks]
                value = sorted_rows[k][at : at + stacks] + pltpu.roll(deep, stacks // 2, 0)
                put_halves(packed, kind * stacks * length + 2 * i + k, stacks, length, value)
        return 0

    lax.fori_loop(0, length // 2, body, 0, unroll=8)
    for half in range(halves):
        inside = slice(half * rows, (half + 1) * rows)
        for kind in range(kinds):
            for part in range(packed.shape[0]):
                at = kind * stacks * length
                block = packed[part, at : at + stacks * length].reshape(stacks, length, 128)
                sent_ref[half, :, kind, 1, :, part * 128 : (part + 1) * 128] = block[:, inside].astype(BF16)
            send(half, kind, 1)
    for copy in sent:
        copy.wait()


def finish_kernel(
    x_ref, arrived_ref, place_ref, land_ref, bottom_ref, result_ref, held, spread, field, arrivals, leaving
):
    kinds, levels, length, width = x_ref.shape
    copies = [pltpu.make_async_copy(x_ref.at[kind], field.at[kind], arrivals.at[kind]) for kind in range(kinds)]
    for copy in copies:
        copy.start()
    halves, stacks, _, _, rows, _ = arrived_ref.shape
    thin = levels - stacks
    each = stacks * kinds * rows
    for half in range(halves):
        for part in range(held.shape[0]):
            block = arrived_ref[half, :, :, 1, :, part * 128 : (part + 1) * 128]
            held[part, half * each : (half + 1) * each] = block.astype(F32).reshape(each, 128)

    def body(i, _):
        half = i // (rows // 2)
        row = 2 * i - half * rows
        cells = []
        for k in range(2):
            for kind in range(kinds):
                cells.append(halves_of(held, half * each + kind * rows + row + k, stacks, kinds * rows))
        cells = jnp.concatenate(cells, axis=0).astype(BF16)
        for k in range(2):
            value = nn(cells, one_hot(place_ref[pl.ds(2 * i + k, 1)]))
            for kind in range(kinds):
                near = (k * kinds + kind) * stacks
                other = ((1 - k) * kinds + kind) * stacks
                at = kind * thin * length + 2 * i + k
                put_halves(spread, at, stacks, length, value[near : near + stacks])
                deep = pltpu.roll(value[other : other + stacks], stacks // 2, 0)
                put_halves(spread, at + stacks * length, stacks, length, deep)
        return 0

    lax.fori_loop(0, length // 2, body, 0, unroll=8)
    depth = jnp.where(land_ref[...] == 1, bottom_ref[...], 0)
    sent = []
    for kind in range(kinds):
        copies[kind].wait()
        for level in range(levels):
            if level < stacks:
                change = jnp.concatenate(
                    [arrived_ref[half, level, kind, 0] for half in range(halves)], axis=0
                ).astype(F32)
            else:
                at = (kind * thin + level - stacks) * length
                change = jnp.concatenate(
                    [spread[part, at : at + length] for part in range(spread.shape[0])], axis=1
                )
            field[kind, level] = jnp.where(level < depth, field[kind, level] + change, 0.0)
            if level % stacks == stacks - 1:
                block = pl.ds(level + 1 - stacks, stacks)
                sent.append(
                    pltpu.make_async_copy(
                        field.at[kind, block], result_ref.at[kind, block], leaving.at[len(sent)]
                    )
                )
                sent[-1].start()
    for copy in sent:
        copy.wait()


def source_kernel(
    rows,
    cells_ref,
    place_ref,
    factors_ref,
    in_ref,
    mid_ref,
    bias_ref,
    out_ref,
    middle_ref,
    spread_ref,
    table_ref,
    held,
):
    _, kinds, width = cells_ref.shape
    ahead = rows + 2
    weights = (in_ref, mid_ref, bias_ref, out_ref)

    def cell(level, row):
        if level == 0:
            return cells_ref[row]
        return spread_ref[(level - 1) * rows + row]

    def spread_out(i):
        row = 2 * i
        cells = jnp.concatenate([cells_ref[rows + row], cells_ref[rows + row + 1]], axis=0)
        for k in range(2):
            table = one_hot(place_ref[row + 2 + k : row + 3 + k])
            table_ref[row + 2 + k] = table
            value = nn(cells, table).astype(BF16)
            spread_ref[row + k] = value[k * kinds : (k + 1) * kinds]
            spread_ref[rows + row + k] = value[(1 - k) * kinds : (2 - k) * kinds]

    def sources(i):
        row = 2 * i
        cells = [cells_ref[row], cells_ref[row + 1], cells_ref[rows + row], cells_ref[rows + row + 1]]
        result = network(jnp.concatenate(cells, axis=1), *[ref[...] for ref in weights])
        held[i] = result.astype(BF16)

    def move(i):
        row = 2 * i
        result = held[i]
        packed = jnp.concatenate(
            [result[:, 2 * width : 3 * width], result[:, 3 * width :]], axis=0
        )
        for k in range(2):
            value = nn(packed, table_ref[row + 2 + k])
            pieces = [
                result[:, k * width : (k + 1) * width].astype(F32),
                value[k * kinds : (k + 1) * kinds],
                value[(1 - k) * kinds : (2 - k) * kinds],
            ]
            for level in range(3):
                factors = factors_ref[level * ahead + row + 1 + k]
                above, below = factors[1:2], factors[2:3]
                if k == 0:
                    above = jnp.where(row > 0, above, 0.0)
                else:
                    below = jnp.where(row + 2 < rows, below, 0.0)
                middle_ref[level * rows + row + k] = advance(
                    cell(level, row + k).astype(F32),
                    cell(level, jnp.maximum(row + k - 1, 0)).astype(F32),
                    cell(level, jnp.minimum(row + k + 1, rows - 1)).astype(F32),
                    pieces[level],
                    factors,
                    above,
                    below,
                )

    def body(i, _):
        move(i - 1)
        sources(i)
        return 0

    for i in range(rows // 2):
        spread_out(i)
    for row in (0, 1, rows + 2, rows + 3):
        table_ref[row] = one_hot(place_ref[row : row + 1])
    sources(0)
    lax.fori_loop(1, rows // 2, body, 0)
    move(rows // 2 - 1)


def step_kernel(
    rows,
    cells_ref,
    spread_ref,
    partial_ref,
    top_ref,
    bottom_ref,
    table_ref,
    factors_ref,
    in_ref,
    mid_ref,
    bias_ref,
    out_ref,
    change_ref,
    middle,
    packed,
    held,
    scratch,
):
    _, kinds, width = cells_ref.shape
    ahead = rows + 2
    weights = (in_ref, mid_ref, bias_ref, out_ref)

    def run(cells):
        return network(jnp.concatenate(cells, axis=1), *[ref[...] for ref in weights]).astype(BF16)

    for level in range(3):
        for row in range(1, rows - 1):
            middle[level * ahead + 1 + row] = partial_ref[level * rows + row]


    def put_together(row, thin):
        values = [nt(thin[k], table_ref[row + 2 + k]) for k in range(2)]
        return [values[k][:kinds] + values[1 - k][kinds:] for k in range(2)]

    def pack(i):
        row = 2 * i
        thin = [
            jnp.concatenate(
                [middle[level * ahead + 1 + row + k].astype(BF16) for level in (1, 2)], axis=0
            )
            for k in range(2)
        ]
        values = put_together(row, thin)
        for k in range(2):
            packed[row + k] = values[k].astype(BF16)

    def sources_of(i):
        row = 2 * i
        cells = [middle[1 + row + k].astype(BF16) for k in range(2)]
        held[i] = run(cells + [packed[row], packed[row + 1]])

    def move(i):
        row = 2 * i
        result = held[i]
        thin_sources = jnp.concatenate(
            [result[:, 2 * width : 3 * width], result[:, 3 * width :]], axis=0
        )
        changes = []
        for k in range(2):
            value = nn(thin_sources, table_ref[row + 2 + k])
            pieces = [
                result[:, k * width : (k + 1) * width].astype(F32),
                value[k * kinds : (k + 1) * kinds],
                value[(1 - k) * kinds : (2 - k) * kinds],
            ]
            for level in range(3):
                at = level * ahead + 1 + row + k
                factors = factors_ref[at]
                value = advance(
                    middle[at],
                    middle[at - 1],
                    middle[at + 1],
                    pieces[level],
                    factors,
                    factors[1:2],
                    factors[2:3],
                )
                if level == 0:
                    first = cells_ref[row + k]
                else:
                    first = spread_ref[(level - 1) * rows + row + k]
                changes.append(value - factors[6:7] * first.astype(F32))
        thin = [
            jnp.concatenate([changes[3 * k + 1].astype(BF16), changes[3 * k + 2].astype(BF16)], axis=0)
            for k in range(2)
        ]
        values = put_together(row, thin)
        for k in range(2):
            put_halves(scratch, row + k, kinds, rows, changes[3 * k])
            put_halves(scratch, rows * kinds + row + k, kinds, rows, values[k])

    def turn(i):
        return (i + 1) % (rows // 2)

    def body(i, _):
        move(turn(i - 1))
        sources_of(turn(i))
        return 0

    for i in range(1, rows // 2 - 1):
        pack(i)
    edges = [
        [top_ref[1], top_ref[2], top_ref[3]],
        [bottom_ref[0], bottom_ref[2], bottom_ref[3]],
    ]
    result = run(edges[0] + edges[1])
    for k in range(2):
        packed_cells = jnp.concatenate(edges[k][1:], axis=0)
        at = 3 * k * width
        packed_sources = jnp.concatenate(
            [result[:, at + width : at + 2 * width], result[:, at + 2 * width : at + 3 * width]], axis=0
        )
        near = nn(jnp.concatenate([packed_cells, packed_sources], axis=0), table_ref[[1, rows + 2][k]])
        far = nn(packed_cells, table_ref[[0, rows + 3][k]])
        near_at = [[1, 0], [0, 1]][k]
        far_at = [[0, 1], [1, 0]][k]
        for level in range(3):
            inside = level * rows + k * (rows - 1)
            if level == 0:
                own = edges[k][0].astype(F32)
                other = (top_ref[0] if k == 0 else bottom_ref[1]).astype(F32)
                sources = result[:, at : at + width].astype(F32)
                inner = cells_ref[k * (rows - 1)].astype(F32)
            else:
                place = near_at[level - 1] * kinds
                own = near[place : place + kinds]
                sources = near[2 * kinds + place : 3 * kinds + place]
                place = far_at[level - 1] * kinds
                other = far[place : place + kinds]
                inner = spread_ref[(level - 1) * rows + k * (rows - 1)].astype(F32)
            row = level * ahead + k * (ahead - 1)
            factors = factors_ref[row]
            middle[row] = advance(
                own,
                other if k == 0 else inner,
                inner if k == 0 else other,
                sources,
                factors,
                factors[1:2],
                factors[2:3],
            )
            row = level * ahead + 1 + k * (rows - 1)
            middle[row] = partial_ref[inside] + factors_ref[row][1 + k : 2 + k] * own
    sources_of(1)
    pack(0)
    pack(rows // 2 - 1)
    lax.fori_loop(1, rows // 2, body, 0, unroll=True)
    move(0)
    for level in range(2):
        for part in range(scratch.shape[0]):
            block = scratch[part, level * rows * kinds : (level + 1) * rows * kinds, :]
            change_ref[:, level, :, part * 128 : (part + 1) * 128] = block.reshape(kinds, rows, 128).astype(BF16)


HBM = pltpu.HBM


def kernel_call(kernel, outs, scratch, flops, name, places=None, result_places=None, memory=32):
    def specs(given):
        return [pl.BlockSpec(memory_space=place or pltpu.VMEM) for place in given]

    spaces = {} if places is None else {"in_specs": specs(places)}
    if result_places is not None:
        given = specs(result_places)
        spaces["out_specs"] = given if isinstance(outs, list) else given[0]
    return pl.pallas_call(
        kernel,
        out_shape=outs,
        **spaces,
        scratch_shapes=scratch,
        cost_estimate=pl.CostEstimate(flops=flops, bytes_accessed=4_000_000, transcendentals=0),
        compiler_params=pltpu.CompilerParams(vmem_limit_bytes=memory * 2**20),
        name=name,
    )


def factors_of(east, north, depth, level):
    wet = (level[:, None, None] < depth[None]).astype(F32)
    opened = time_step * wet[:, :-1] * wet[:, 1:]
    plus = opened * (jnp.maximum(east[:, :-1], 0.0) + diffusion)
    minus = opened * (jnp.minimum(east[:, :-1], 0.0) - diffusion)
    inner = wet[:, 1:-1]
    flow = jnp.pad(north[:, 1:-1], ((0, 0), (0, 0), (1, 0)))
    sides = jnp.pad(inner, ((0, 0), (0, 0), (1, 1)))
    opened = time_step * sides[..., :-1] * sides[..., 1:]
    right = opened * (jnp.maximum(flow, 0.0) + diffusion)
    left = opened * (jnp.minimum(flow, 0.0) - diffusion)
    own = inner + (minus[:, :-1] - plus[:, 1:]) + (left[..., :-1] - right[..., 1:])
    return jnp.stack(
        [
            own,
            plus[:, :-1],
            -minus[:, 1:],
            right[..., :-1],
            -left[..., 1:],
            time_step * inner,
            inner,
            jnp.zeros_like(inner),
        ],
        axis=2,
    )


def with_halo(value, sides, width):
    for axis, dim in sides:
        size, length = (lax.axis_size(axis), value.shape[dim])
        up = [(i, (i + 1) % size) for i in range(size - 1)]
        down = [(j, i) for i, j in up]
        last = lax.slice_in_dim(value, length - width, length, axis=dim)
        initial = lax.slice_in_dim(value, 0, width, axis=dim)
        before = lax.ppermute(last, axis, up)
        after = lax.ppermute(initial, axis, down)
        value = jnp.concatenate([before, value, after], axis=dim)
    return value


def as_sent(value):
    return jax.tree.map(lambda a: a.astype(jnp.bfloat16) if a.dtype == jnp.float32 else a, value)


def face_flux(behind_cells, ahead_cells, flow_speed, opened):
    moved = jnp.maximum(flow_speed, 0.0) * behind_cells + jnp.minimum(flow_speed, 0.0) * ahead_cells
    return opened * (moved - diffusion * (ahead_cells - behind_cells))


def plain_network(inputs, in_weight, in_bias, mid_weight, mid_bias, out_weight):
    kinds, depth, rows, cols = inputs.shape
    cells = depth * rows * cols
    turns = math.gcd(cells, 8)
    blocked = jnp.moveaxis(inputs.reshape(kinds, turns, cells // turns), 1, 0)

    def one_block(cell_block):
        first_hidden = (
            jnp.einsum("tn,th->nh", cell_block, in_weight, preferred_element_type=jnp.float32)
            + in_bias
        )
        first_hidden = jax.nn.silu(first_hidden).astype(jnp.bfloat16)
        second_hidden = (
            jnp.einsum("nh,hk->nk", first_hidden, mid_weight, preferred_element_type=jnp.float32)
            + mid_bias
        )
        second_hidden = jax.nn.silu(second_hidden).astype(jnp.bfloat16)
        return jnp.einsum(
            "nh,ht->tn", second_hidden, out_weight, preferred_element_type=jnp.float32
        ).astype(jnp.bfloat16)

    result = jnp.moveaxis(lax.map(one_block, blocked), 0, 1)
    return result.reshape(result.shape[0], depth, rows, cols)


def plain_body(
    tracers,
    east_speed,
    north_speed,
    land_mask,
    bottom_level,
    in_weight,
    in_bias,
    mid_weight,
    mid_bias,
    out_weight,
):
    levels = east_speed.shape[0]
    depth = jnp.arange(levels, dtype=jnp.int32)[:, None, None]
    wet_cells = ((land_mask[None] == 1) & (depth < bottom_level[None])).astype(jnp.float32)
    geometry = with_halo(
        jnp.stack([east_speed, wet_cells]).astype(jnp.bfloat16), (("tile", 2),), 1
    ).astype(jnp.float32)
    flow_x = geometry[0, :, :-1]
    wet_x = geometry[1]
    opened_x = wet_x[:, :-1] * wet_x[:, 1:]
    flow_y = jnp.pad(north_speed, ((0, 0), (0, 0), (1, 0)))
    wet_y = jnp.pad(wet_cells, ((0, 0), (0, 0), (1, 1)))
    opened_y = wet_y[..., :-1] * wet_y[..., 1:]
    field = tracers
    for step in range(STEPS):
        padded = with_halo(as_sent(field), (("tile", 2),), 1).astype(field.dtype)
        inputs = field.astype(jnp.bfloat16)
        local_sources = plain_network(
            lax.all_to_all(inputs, "tracer", split_axis=2, concat_axis=0, tiled=True),
            in_weight,
            in_bias,
            mid_weight,
            mid_bias,
            out_weight,
        )
        sources = lax.all_to_all(local_sources, "tracer", split_axis=0, concat_axis=2, tiled=True)
        x_flux = face_flux(padded[:, :, :-1], padded[:, :, 1:], flow_x, opened_x)
        cells_y = jnp.pad(field, ((0, 0), (0, 0), (0, 0), (1, 1)))
        y_flux = face_flux(cells_y[..., :-1], cells_y[..., 1:], flow_y, opened_y)
        tendency = x_flux[:, :, :-1] - x_flux[:, :, 1:] + (y_flux[..., :-1] - y_flux[..., 1:])
        field = wet_cells[None] * (field + time_step * (tendency + sources.astype(jnp.float32)))
    return field


def split_parts(value, count):
    parts = []
    for _ in range(count):
        parts.append(value.astype(BF16))
        value = value - parts[-1].astype(F32)
    return parts


def body(
    tracers,
    east_speed,
    north_speed,
    land_mask,
    bottom_level,
    in_weight,
    in_bias,
    mid_weight,
    mid_bias,
    out_weight,
):
    arguments = (
        tracers,
        east_speed,
        north_speed,
        land_mask,
        bottom_level,
        in_weight,
        in_bias,
        mid_weight,
        mid_bias,
        out_weight,
    )
    kinds, levels, length, columns = tracers.shape
    tiles, group = lax.axis_size("tile"), lax.axis_size("tracer")
    halves = 2
    stacks = group // halves
    rows = length // halves
    own = lax.axis_index("tracer")
    half, stack = own // stacks, own % stacks
    all_kinds = kinds * group
    thin = levels - stacks
    parts = columns // 128

    sent, place = kernel_call(
        pack_kernel,
        [
            jax.ShapeDtypeStruct((halves, stacks, kinds, 2, rows, columns), BF16),
            jax.ShapeDtypeStruct((length, columns), F32),
        ],
        [
            pltpu.VMEM((length, columns), F32),
            pltpu.VMEM((length * 32, 2 * columns), BF16),
            pltpu.VMEM((2 * columns, columns), BF16),
            pltpu.VMEM((parts, (kinds * thin + 1) * length, 128), F32),
            pltpu.VMEM((kinds, stacks * length, columns), F32),
            pltpu.VMEM((parts, (kinds * stacks + 1) * length, 128), F32),
            pltpu.VMEM((length, columns), jnp.int32),
            pltpu.VMEM((length, columns), jnp.int32),
            pltpu.VMEM((halves, stacks, kinds, 2, rows, columns), BF16),
            pltpu.SemaphoreType.DMA((kinds * parts + 3,)),
            pltpu.SemaphoreType.DMA((halves * kinds * 2,)),
        ],
        2 * length * columns * columns * (32 + 64),
        "pack",
        [HBM, HBM, HBM],
        [HBM, None],
    )(tracers.reshape(kinds, levels * length, columns), land_mask, bottom_level)
    sent = sent.reshape(group, kinds, 2, rows, columns)
    cells = lax.all_to_all(sent, "tracer", split_axis=0, concat_axis=0, tiled=True)
    cells = cells.reshape(all_kinds, 2, rows, columns)

    east_speed, north_speed, land_mask, sent = lax.optimization_barrier(
        (east_speed, north_speed, land_mask, sent)
    )
    depth = jnp.where(land_mask == 1, bottom_level, 0).astype(F32)
    level_list = [stack, stacks + stack, 2 * stacks + (stack + stacks // 2) % stacks]

    side, position = stack // (stacks // 2), stack % (stacks // 2)

    def own_levels(value):
        value = value.reshape(2 * levels // stacks, stacks // 2, length, columns)
        value = lax.dynamic_slice_in_dim(value, position, 1, 1)[:, 0]
        return jnp.where(
            side == 0,
            jnp.stack([value[0], value[2], value[5]]),
            jnp.stack([value[1], value[3], value[4]]),
        )

    geometry = [own_levels(east_speed), own_levels(north_speed), depth[None], place[None]]

    def at(tile, part, position):
        return tile * group + part * stacks + position

    across, within = [], []
    for position in range(stacks):
        for tile in range(tiles):
            within.append((at(tile, 0, position), at(tile, 1, position)))
            if tile + 1 < tiles:
                across.append((at(tile, 1, position), at(tile + 1, 0, position)))
    back = [(j, i) for i, j in across]
    axes = ("tile", "tracer")
    edge = jnp.concatenate(
        [lax.dynamic_slice_in_dim(value, half * (length - 2), 2, 1) for value in geometry], axis=0
    )
    arrived = lax.ppermute(edge, axes, across + back)
    arrived = [arrived[:3], arrived[3:6], arrived[6:7], arrived[7:8]]

    def widened(value, outside):
        return jnp.where(
            half == 0,
            jnp.concatenate([outside, value[:, : rows + 2]], axis=1),
            jnp.concatenate([value[:, rows - 2 :], outside], axis=1),
        )

    east, north, wide_depth, wide_place = [widened(*pair) for pair in zip(geometry, arrived)]
    factors = factors_of(east, north, wide_depth[0], jnp.stack(level_list).astype(F32)).reshape(
        3 * (rows + 2), 8, columns
    )

    level = jnp.arange(levels, dtype=jnp.int32).astype(F32)
    count = jnp.sum((level[:, None, None] < depth[None]).astype(F32), axis=2)
    deep = jnp.roll(count[2 * stacks :], -(stacks // 2), axis=0)
    deep = jnp.flip(deep.reshape(stacks, length // 2, 2), axis=2).reshape(stacks, length)
    fullest = count[stacks : 2 * stacks] + deep
    fullest, cells = lax.optimization_barrier((fullest, cells))

    in_parts = jnp.stack(split_parts(0.5 * in_bias, 3) + [jnp.zeros(in_bias.shape, BF16)] * 13, axis=1)
    weights = (
        jnp.concatenate([(0.5 * in_weight.astype(F32)).astype(BF16).T, in_parts], axis=1),
        (0.5 * mid_weight.astype(F32)).astype(BF16).T,
        jnp.broadcast_to(0.5 * mid_bias[:, None], mid_bias.shape + (128,)),
        out_weight.T,
    )

    hidden = in_weight.shape[1]
    pieces = 2 * rows
    per_piece = 2 * columns * hidden * (hidden + 2 * all_kinds)
    turned, first, last = kernel_call(
        functools.partial(turn_kernel, rows),
        [
            jax.ShapeDtypeStruct((pieces, all_kinds, columns), BF16),
            jax.ShapeDtypeStruct((4, all_kinds, columns), BF16),
            jax.ShapeDtypeStruct((4, all_kinds, columns), BF16),
        ],
        [pltpu.VMEM((parts, (all_kinds + 1) * rows, 128), F32)],
        1_000_000,
        "turn",
    )(cells)
    top = lax.ppermute(last, axes, within + across)
    bottom = lax.ppermute(first, axes, [(j, i) for i, j in within] + back)
    partial, spread, table = kernel_call(
        functools.partial(source_kernel, rows),
        [
            jax.ShapeDtypeStruct((3 * rows, all_kinds, columns), F32),
            jax.ShapeDtypeStruct((2 * rows, all_kinds, columns), BF16),
            jax.ShapeDtypeStruct((rows + 4, columns, columns), BF16),
        ],
        [pltpu.VMEM((rows // 2, all_kinds, 4 * columns), BF16)],
        pieces * per_piece,
        "sources",
    )(turned, wide_place[0], factors, *weights)
    change = kernel_call(
        functools.partial(step_kernel, rows),
        jax.ShapeDtypeStruct(cells.shape, BF16),
        [
            pltpu.VMEM((3 * (rows + 2), all_kinds, columns), F32),
            pltpu.VMEM((rows, all_kinds, columns), BF16),
            pltpu.VMEM((rows // 2, all_kinds, 4 * columns), BF16),
            pltpu.VMEM((parts, (2 * all_kinds + 1) * rows, 128), F32),
        ],
        pieces * per_piece,
        "steps",
    )(turned, spread, partial, top, bottom, table, factors, *weights)

    fullest, change = lax.optimization_barrier((fullest, change))
    for step in (1, tiles // 4):
        others = []
        for times in (1, 2, 3):
            pairs = [(tile, tile ^ (step * times)) for tile in range(tiles)]
            others.append(lax.ppermute(fullest, "tile", pairs))
        fullest = functools.reduce(jnp.maximum, others, fullest)
    excess = jnp.max(fullest) > columns

    change = change.reshape(group, kinds, 2, rows, columns)
    change = lax.all_to_all(change, "tracer", split_axis=0, concat_axis=0, tiled=True)
    change = change.reshape(halves, stacks, kinds, 2, rows, columns)

    def finish(change, place, arguments):
        return kernel_call(
            finish_kernel,
            jax.ShapeDtypeStruct(tracers.shape, F32),
            [
                pltpu.VMEM((parts, (group + 1) * kinds * rows, 128), F32),
                pltpu.VMEM((parts, (kinds * thin + 1) * length, 128), F32),
                pltpu.VMEM(tracers.shape, F32),
                pltpu.SemaphoreType.DMA((kinds,)),
                pltpu.SemaphoreType.DMA((kinds * levels // stacks,)),
            ],
            2 * length * columns * columns * 32,
            "finish",
            [HBM, None, None, None, None],
            [HBM],
            memory=63,
        )(arguments[0], change, place, arguments[3], arguments[4])

    def in_full(change, place, arguments):
        return plain_body(*arguments)

    return lax.cond(excess, in_full, finish, change, place, arguments)


def solution(mesh):
    return jax.shard_map(
        body,
        mesh=mesh,
        in_specs=(
            P("tracer", None, "tile", None),
            P(None, "tile", None),
            P(None, "tile", None),
            P("tile", None),
            P("tile", None),
            P(),
            P(),
            P(),
            P(),
            P(),
        ),
        out_specs=P("tracer", None, "tile", None),
        check_vma=False,
    )
```
